768 devices in a mesh: row: 48 (over z, x), col: 16 (over y, core).
Axes of the slice: x: 4, y: 8, z: 12, core: 2. Of those that a mesh axis runs over, the one named last changes fastest.
Arguments:
- amplitudes: bfloat16 [96, 128, 128, 128], P('row', 'col'), may hold values from -6 to 6
- amplitude_mask: int32 [96, 128], P('row', 'col'), may hold values 0 or 1
- integrals: bfloat16 [48, 128, 128, 128], P('row', 'col'), may hold values from -0.046875 to 0.046875
- integral_mask: int32 [48, 128], P('row', 'col'), may hold values from 0 to 1, as said below
- owners: int32 [48, 1], replicated, may hold values from 0 to 15; in each aligned block of 48 rows (0 to 47, 48 to 95, ...) at most 4 rows name the same one
Outputs:
- residual: bfloat16 [96, 64, 128, 128], P('row', 'col')
The draws below stay inside these ranges and needn't reach their ends.
Inputs may be any that keep to these rules, and one draw needn't show every extreme that they name: `integral_mask`: among the 8 cd tiles that one device holds of its ab tile at most 4 are 1, and exactly 4 on some devices. `owners`: each col index owns at least one and at most 4 ab tiles; one owns exactly 4.
All inputs are finite; a program needn't handle non-finite values. No bound on the sum of `amplitude_mask` on one device may be relied on, other than what follows from the above.
Results may differ from the reference program's by a relative error of at most 0.022.
Values may be sent and summed in bfloat16 or wider, within the bound.
A program may use at most 64 MiB of HBM per device.

```python
import math
import jax
import jax.numpy as jnp
import numpy as np
from jax import lax

B = 128
C_DEV = 8
V_MOST = 4
NA = 48
NI = 96
NC = 128
SLOTS = 4
N_COL = 16


def draw_integral_mask(key, part):
    key = jax.random.fold_in(key, 7)
    first_key, second_key = jax.random.split(key)
    groups = NC // C_DEV
    counts = jax.random.randint(first_key, (NA, groups, 1), 1, V_MOST + 1)
    counts = counts.at[0].set(V_MOST)
    scores = jax.random.randint(second_key, (NA, groups, C_DEV), 0, 1048576) * C_DEV + jnp.arange(C_DEV, dtype=jnp.int32)
    ranks = jnp.argsort(jnp.argsort(scores, axis=-1), axis=-1)
    return (ranks < counts).astype(jnp.int32).reshape(NA, NC)


def plant(result, rng, least, top_value):
    longest = result.shape.index(max(result.shape))
    spots = []
    for shift in (0, 1):
        where = [jax.random.randint(jax.random.fold_in(rng, axis), (), 0, length) for axis, length in enumerate(result.shape)]
        where[longest] = (where[longest] + shift) % result.shape[longest]
        spots.append(tuple(where))
    return result.at[spots[0]].set(least).at[spots[1]].set(top_value)


def steps_of(key, shape, shards, low, high):
    def one(axis_at, blocks):
        steps = jax.random.uniform(jax.random.fold_in(jax.random.fold_in(key, 6), axis_at), (blocks,), jnp.float32, low / len(shards), high / len(shards))
        return jnp.repeat(jnp.exp(steps), shape[axis_at] // blocks).reshape((-1,) + (1,) * (len(shape) - axis_at - 1))

    level = one(*shards[0])
    for cut in shards[1:]:
        level = level * one(*cut)
    return level


def routed_block(rng, own, number, rows, count, top, reach, lean):
    sequence = jax.random.permutation(rng, count)
    crowded, common = portions_of(count, rows * top, reach, lean, True), portions_of(count, rows * top, reach, lean, False)
    places = jnp.arange(count)

    def named(tallies, offset_by):
        used = int((tallies > 0).sum())
        fixed = max(1, used // 4)
        shifted = fixed + (places - fixed + offset_by * (used - fixed)) % max(1, count - fixed)
        return jnp.zeros((count,), jnp.int32).at[sequence[jnp.where(places < fixed, places, shifted)]].set(jnp.asarray(tallies, jnp.int32))

    tallies = jnp.where(number % 4 == 0, named(crowded, number // 4), named(common, number - number // 4 - 1))
    mixed = jax.random.permutation(jax.random.fold_in(own, 3), count)
    giver, receiver = mixed[0:count // 2 * 2:2], mixed[1:count // 2 * 2:2]
    margin = jnp.minimum(tallies[giver] - 1, reach - tallies[receiver]) // 2
    margin = jnp.where((giver == sequence[0]) | (receiver == sequence[0]) | (tallies[receiver] == 0), 0, jnp.maximum(margin, 0))
    shifted = jax.random.randint(jax.random.fold_in(own, 4), (count // 2,), 0, 1 << 20) % (margin + 1)
    tallies = tallies.at[giver].add(-shifted).at[receiver].add(shifted)
    labels = jnp.searchsorted(jnp.cumsum(tallies), jnp.arange(rows * top), side="right").astype(jnp.int32)
    grid = labels.reshape(top, rows).T
    grid = grid[jax.random.permutation(jax.random.fold_in(own, 1), rows)]
    offset_by = jax.random.randint(jax.random.fold_in(own, 2), (rows, 1), 0, top)
    return jnp.take_along_axis(grid, (jnp.arange(top)[None, :] + offset_by) % top, axis=1)


def portions_of(number_of, total, most, slope, full):
    portions = [(1 << 20) // math.isqrt(grade ** slope) + 1 for grade in range(1, number_of + 1)]
    largest = most if full else min(most, max(-(-total // number_of), total * portions[0] // sum(portions)))
    least = 1 if total - largest >= number_of - 1 else 0
    given, spare = [largest] + [least] * (number_of - 1), total - largest - least * (number_of - 1)
    while spare > 0:
        candidates = [i for i in range(1, number_of) if given[i] < largest] or [i for i in range(1, number_of) if given[i] < most]
        pool, left = sum([portions[i] for i in candidates]), spare
        for i in candidates:
            addition = min(most - given[i], max(1, left * portions[i] // pool), spare)
            given[i] = given[i] + addition
            spare = spare - addition
    return np.array(given)


def bell_draw(key, dims, spread, bound, cuts=(), kind=jnp.bfloat16):
    gain = steps_of(key, dims, cuts, -0.22, 0.18) if cuts else 1.0
    result = jax.random.normal(key, dims, jnp.float32) * spread * gain
    return jnp.minimum(jnp.maximum(result, -bound), bound).astype(kind)


def setup_inputs(seed: int = 0) -> dict:
    key_list = jax.random.split(jax.random.key(seed), 6)
    amplitudes = bell_draw(key_list[0], (NI, NC, B, B), 1.0, 6.0, ((0, 48), (1, 16)))
    amplitude_mask = plant((jax.random.randint(key_list[1], (NI, NC), 0, 4) < 3).astype(jnp.int32), jax.random.fold_in(key_list[1], 1), 0, 1)
    integrals = bell_draw(key_list[2], (NA, NC, B, B), (NC * B) ** -0.5, 0.046875, ((0, 48), (1, 16)))
    integral_mask = draw_integral_mask(jax.random.fold_in(key_list[5], 71), 0)
    owners_keys = jax.random.split(jax.random.fold_in(key_list[4], 1), NA // NA)
    owners_turns = jax.random.permutation(jax.random.fold_in(key_list[4], 3), NA // NA)
    owners = jax.vmap(lambda own, number: routed_block(jax.random.fold_in(key_list[4], 2), own, number, NA, N_COL, 1, SLOTS, 2))(owners_keys, owners_turns).reshape((NA, 1))
    return {"amplitudes": amplitudes, "amplitude_mask": amplitude_mask, "integrals": integrals, "integral_mask": integral_mask, "owners": owners}


def slot_numbers(owners):
    owner_list = owners[:, 0]
    count = owner_list.shape[0]
    positions = jnp.arange(count, dtype=jnp.int32)
    earlier = (owner_list[None, :] == owner_list[:, None]) & (positions[None, :] < positions[:, None])
    ranks = jnp.sum(earlier.astype(jnp.int32), axis=1).astype(jnp.int32)
    return (owner_list * SLOTS + ranks).astype(jnp.int32)


def reference(amplitudes, amplitude_mask, integrals, integral_mask, owners):
    amp_kept = amplitudes * amplitude_mask[:, :, None, None].astype(jnp.bfloat16)
    int_kept = integrals * integral_mask[:, :, None, None].astype(jnp.bfloat16)
    groups = NC // C_DEV
    int_float = int_kept.reshape(NA, groups, C_DEV, B, B).astype(jnp.float32)

    def one_row(amp_row):
        amp_float = amp_row.reshape(groups, C_DEV, B, B).astype(jnp.float32)
        partial_value = jnp.einsum("gcxy,sgcwy->gsxw", amp_float, int_float)
        rounded = lax.optimization_barrier(partial_value.astype(jnp.bfloat16))
        return jnp.sum(rounded.astype(jnp.float32), axis=0)

    ladder = lax.map(one_row, amp_kept)
    slots = slot_numbers(owners)
    residual = jnp.zeros((NI, N_COL * SLOTS, B, B), jnp.float32)
    residual = residual.at[:, slots].set(ladder)
    return residual.astype(jnp.bfloat16)
```

```python
import functools

import jax
import jax.numpy as jnp
from jax import lax
from jax.experimental import pallas as pl
from jax.experimental.pallas import tpu as pltpu
from jax.sharding import PartitionSpec as P


B = 128
X = 4
C = 8
V = 4
META = 16
UNIT = V * B + META
HALF = 256
F32 = jnp.float32
BF16 = jnp.bfloat16
I32 = jnp.int32


def orbit_colour(left, right, eye, row, col):
    step = jnp.dot(right.astype(BF16), left.astype(BF16), preferred_element_type=F32)
    reach = jnp.minimum(step + eye, 1.0)
    for _ in range(5):
        half = reach.astype(BF16)
        reach = jnp.minimum(jnp.dot(half, half, preferred_element_type=F32), 1.0)
    label_r = jnp.min(jnp.where(reach > 0.5, row, 999.0), axis=0, keepdims=True)
    label_c = jnp.min(jnp.where(reach > 0.5, col, 999.0), axis=1, keepdims=True)
    other_r = jnp.sum(left * label_c, axis=0, keepdims=True)
    other_c = jnp.sum(left * label_r, axis=1, keepdims=True)
    return jnp.where(label_r > other_r, 1.0, 0.0), jnp.where(label_c > other_c, 1.0, 0.0)


def flip(value):
    return value + 1.0 - 2.0 * (value - 2.0 * jnp.floor(value * 0.5))


def colours_of(owners):
    n = owners.shape[0]
    row_i = lax.broadcasted_iota(I32, (n, n), 0)
    col_i = lax.broadcasted_iota(I32, (n, n), 1)
    row, col = row_i.astype(F32), col_i.astype(F32)
    one = lambda cond: jnp.where(cond, 1.0, 0.0)
    eye = one(row_i == col_i)
    before_r, before_c = one(row_i < col_i), one(col_i < row_i)
    own_c = jnp.broadcast_to(owners, (n, n))
    own_r = jnp.sum(own_c * eye, axis=0, keepdims=True)
    same = one(own_c == own_r)
    over0 = lambda v: jnp.sum(v, axis=0, keepdims=True)
    over1 = lambda v: jnp.sum(v, axis=1, keepdims=True)
    rank_r, rank_c = over0(same * before_r), over1(same * before_c)
    count_r, count_c = over0(same), over1(same)
    even_r, even_c = one(flip(rank_r) > rank_r), one(flip(rank_c) > rank_c)
    lone_r, lone_c = even_r * one(rank_r == count_r - 1.0), even_c * one(rank_c == count_c - 1.0)
    nth_r, nth_c = over0(lone_c * before_r), over1(lone_r * before_c)
    left = one(row_i == (col_i ^ 1))
    right = same * one(rank_c == flip(rank_r)) + lone_c * lone_r * one(nth_c == flip(nth_r))
    first_r, first_c = orbit_colour(left, right, eye, row, col)
    alike = one(first_c == first_r)
    apart = 1.0 - eye
    left = one((row_i // X) == (col_i // X)) * alike * apart
    right = same * alike * apart
    lone_r, lone_c = 1.0 - over0(right), 1.0 - over1(right)
    nth_r, nth_c = over0(lone_c * alike * before_r), over1(lone_r * alike * before_c)
    right = right + lone_c * lone_r * alike * one(nth_c == flip(nth_r))
    second_r, _ = orbit_colour(left, right, eye, row, col)
    return 2.0 * first_r + second_r, rank_r, own_r


TABLE = 40


def table_of(owners, me_x, me_z, me_col, cols):
    colour, rank, own = colours_of(owners.astype(F32))
    n = owners.shape[0]

    def part(rows, make):
        at = lax.broadcasted_iota(I32, (rows, n), 0).astype(F32)
        edge = lax.broadcasted_iota(I32, (rows, n), 1)
        return jnp.sum(make(at, (edge // X).astype(F32), (edge % X).astype(F32)), axis=1, keepdims=True)

    x, z, d = me_x.astype(F32), me_z.astype(F32), me_col.astype(F32)
    slots = part(cols, lambda at, ez, ex: jnp.where((own == at) & (colour == x), ez + 1.0, 0.0))
    mine = part(8, lambda at, ez, ex: jnp.where((rank == at) & (own == d), colour + 1.0, 0.0))
    unit = part(8, lambda at, ez, ex: jnp.where((colour == x) & (ez == z), ex, 0.0))
    spare = jnp.zeros((TABLE - cols - 16, 1), F32)
    rows = jnp.concatenate([slots, mine, unit, spare], axis=0)
    return jnp.broadcast_to(rows, (TABLE, 128)).astype(I32)


def kernel(
    Z, Y, amp, amp_mask, integral, int_mask, owners, out,
    A, XI, G, mine, part_out, part_in, ring_out, ring_in, met, table_v, table_s, meta_v, meta_s,
    xi_send, xi_recv, a_send, a_recv, z_send, z_recv, p_send, p_recv, r_send, r_recv, m_send, m_recv, local,
):
    row, col = lax.axis_index("row"), lax.axis_index("col")
    x, z, y, core = row % X, row // X, col // 2, col % 2

    def at_x(shift):
        return (z * X + (x + shift) % X, col)

    def at_z(shift):
        return (((z + shift) % Z) * X + x, col)

    def at_y(shift):
        return (row, ((y + shift) % Y) * 2 + core)

    partner = (row, y * 2 + (1 - core))

    barrier = pltpu.get_barrier_semaphore()
    peers = [at_x(1), at_x(2), at_x(3), at_z(1), at_z(Z - 1), at_y(1), at_y(Y - 1), partner]
    for peer in peers:
        pl.semaphore_signal(barrier, inc=1, device_id=peer, device_id_type=pl.DeviceIdType.MESH)

    def copy(src, dst, send, recv, to):
        return pltpu.make_async_remote_copy(
            src_ref=src, dst_ref=dst, send_sem=send, recv_sem=recv, device_id=to,
            device_id_type=pl.DeviceIdType.MESH,
        )

    kept = [int_mask[0, c] for c in range(C)]
    before, places = jnp.int32(0), [jnp.int32(0)] * V
    for c in range(C):
        for j in range(V):
            places[j] = jnp.where((kept[c] != 0) & (before == j), c, places[j])
        before = before + kept[c]
    for j in range(V):
        scale = jnp.where(before > j, 1.0, 0.0).astype(BF16)
        XI[0, j * B:(j + 1) * B, :] = integral[0, places[j]] * scale
    at = lax.broadcasted_iota(I32, (META, B), 0)
    meta = jnp.zeros((META, B), I32)
    for j in range(V):
        meta = jnp.where(at == j, places[j], meta)
    XI[0, V * B:UNIT, :] = meta.astype(F32).astype(BF16)

    pl.semaphore_wait(barrier, len(peers))

    xi_right = copy(XI.at[0], XI.at[3], xi_send.at[0], xi_recv.at[0], at_x(1))
    xi_left = copy(XI.at[0], XI.at[1], xi_send.at[1], xi_recv.at[1], at_x(3))
    xi_right.start()
    xi_left.start()

    for i in range(2):
        for c in range(C):
            A[i, c] = amp[i, c] * amp_mask[i, c].astype(F32).astype(BF16)

    a_copies = [
        copy(A.at[0], A.at[6], a_send.at[0], a_recv.at[0], at_x(1)),
        copy(A.at[1], A.at[3], a_send.at[1], a_recv.at[1], at_x(3)),
        copy(A.at[1], A.at[7], a_send.at[2], a_recv.at[2], at_x(1)),
        copy(A.at[0], A.at[2], a_send.at[3], a_recv.at[3], at_x(3)),
    ]
    a_on_right = copy(A.at[6], A.at[4], a_send.at[4], a_recv.at[4], at_x(1))
    a_on_left = copy(A.at[3], A.at[5], a_send.at[5], a_recv.at[5], at_x(3))

    table_v[...] = table_of(owners[...], x, z, col, 2 * Y)
    table_copy = pltpu.make_async_copy(table_v, table_s, local.at[0])
    table_copy.start()

    xi_on_right = copy(XI.at[3, 0:HALF], XI.at[2, 0:HALF], xi_send.at[2], xi_recv.at[2], at_x(1))
    xi_on_left = copy(XI.at[1, HALF:UNIT], XI.at[2, HALF:UNIT], xi_send.at[3], xi_recv.at[3], at_x(3))
    xi_right.wait_recv()
    xi_on_right.start()
    xi_left.wait_recv()
    xi_on_left.start()
    for c in a_copies:
        c.start()
    table_copy.wait()
    xi_on_right.wait_recv()
    xi_on_left.wait_recv()

    G[0] = XI[(jnp.clip(table_s[2 * Y + 8, 0], 0, X - 1) - x + X) % X]

    def meta_out(rel):
        meta_v[rel] = G[rel, V * B:UNIT, :].astype(F32).astype(I32)[0:8]
        pltpu.make_async_copy(meta_v.at[rel], meta_s.at[rel], local.at[1 + rel]).start()

    steps = Z // 2 - 1
    to_right, to_left = [], []
    for s in range(steps):
        to_right.append(copy(G.at[(Z - s) % Z], G.at[Z - 1 - s], z_send.at[0, s], z_recv.at[0, s], at_z(1)))
        to_left.append(copy(G.at[s], G.at[s + 1], z_send.at[1, s], z_recv.at[1, s], at_z(Z - 1)))
    far = Z // 2
    to_right.append(copy(
        G.at[far + 1, 0:HALF], G.at[far, 0:HALF], z_send.at[0, steps], z_recv.at[0, steps], at_z(1)))
    to_left.append(copy(
        G.at[far - 1, HALF:UNIT], G.at[far, HALF:UNIT], z_send.at[1, steps], z_recv.at[1, steps], at_z(Z - 1)))

    to_right[0].start()
    to_left[0].start()
    meta_out(0)
    for s in range(steps):
        to_right[s].wait_recv()
        to_right[s + 1].start()
        to_left[s].wait_recv()
        to_left[s + 1].start()
        meta_out(Z - 1 - s)
        meta_out(s + 1)
        if s == 2:
            a_copies[0].wait_recv()
            a_on_right.start()
            a_copies[1].wait_recv()
            a_on_left.start()
    to_right[steps].wait_recv()
    to_left[steps].wait_recv()
    meta_out(far)
    a_copies[2].wait_recv()
    a_copies[3].wait_recv()
    a_on_right.wait_recv()
    a_on_left.wait_recv()
    for rel in range(Z):
        pltpu.make_async_copy(meta_v.at[rel], meta_s.at[rel], local.at[1 + rel]).wait()

    FLOW = ((0, 1), (3, 2))

    def part_copy(s):
        return copy(part_out.at[s], part_in.at[s], p_send.at[s], p_recv.at[s], partner)

    def ring_copy(s, way, sub):
        return copy(
            ring_out.at[s, way, sub], ring_in.at[s + 1, way, sub], r_send.at[s, way, sub], r_recv.at[s, way, sub],
            at_y(1 if way == 0 else Y - 1),
        )

    def products(s):
        for way in range(2):
            slot_y = (y - 1 - s + 2 * Y) % Y if way == 0 else (y + 1 + s) % Y
            for whose in (1, 0):
                owner = slot_y * 2 + (core if whose == 0 else 1 - core)
                named = table_s[owner, 0]
                filled = jnp.where(named > 0, 1.0, 0.0).astype(F32)
                rel = jnp.clip(named - 1, 0, Z - 1) - z
                rel = jnp.where(rel < 0, rel + Z, rel)
                where = [jnp.clip(meta_s[rel, j, 0], 0, C - 1) for j in range(V)]
                unit = G[rel, 0:V * B, :]
                pairs = [
                    jnp.concatenate([unit[j * B:(j + 1) * B], unit[(j + 1) * B:(j + 2) * B]], axis=1)
                    for j in range(0, V, 2)
                ]
                for sub in range(2):
                    r = FLOW[way][sub]
                    total = None
                    for p, pair in enumerate(pairs):
                        tiles = jnp.concatenate(
                            [A[2 * r:2 * r + 2, where[2 * p + q]].reshape(2 * B, B) for q in range(2)], axis=1)
                        term = lax.dot_general(tiles, pair, (((1,), (1,)), ((), ())), preferred_element_type=F32)
                        total = term if total is None else total + term
                    total = total * filled
                    if whose == 0:
                        mine[s, way, sub] = total
                    else:
                        part_out[s, way, sub] = total.astype(BF16)
        part_copy(s).start()

    ring_in[0] = jnp.zeros_like(ring_in[0])
    products(0)

    def ring_step(s, carry):
        part_copy(s).wait_recv()
        for sub in range(2):
            for way in range(2):
                @pl.when(s > 0)
                def _():
                    ring_copy(s - 1, way, sub).wait_recv()
                total = mine[s, way, sub] + part_in[s, way, sub].astype(F32) + ring_in[s, way, sub].astype(F32)
                ring_out[s, way, sub] = total.astype(BF16)
                ring_copy(s, way, sub).start()
        products(s + 1)
        return carry

    lax.fori_loop(0, Y - 1, ring_step, jnp.int32(0))

    def met_copy(r):
        return copy(ring_out.at[Y - 1, *PLACE[r]], met.at[X - r], m_send.at[r - 1], m_recv.at[r - 1], at_x(r))

    PLACE = {FLOW[way][sub]: (way, sub) for way in range(2) for sub in range(2)}
    last = Y - 1
    part_copy(last).wait_recv()
    for sub in range(2):
        for way in range(2):
            r = FLOW[way][sub]
            ring_copy(last - 1, way, sub).wait_recv()
            total = mine[last, way, sub] + part_in[last, way, sub].astype(F32) + ring_in[last, way, sub].astype(F32)
            if r == 0:
                met[0] = total.astype(BF16)
            else:
                ring_out[last, way, sub] = total.astype(BF16)
                met_copy(r).start()
    for r in range(1, X):
        met_copy(r).wait_recv()
    slots = out.shape[1]
    for t in range(slots):
        named = table_s[2 * Y + t, 0]
        filled = jnp.where(named > 0, 1.0, 0.0).astype(BF16)
        rel = jnp.clip(named - 1, 0, X - 1) - x
        tiles = met[jnp.where(rel < 0, rel + X, rel)] * filled
        for i in range(2):
            out[i, t] = tiles[i * B:(i + 1) * B]

    for c in [xi_right, xi_left, xi_on_right, xi_on_left, *a_copies, a_on_right, a_on_left, *to_right, *to_left]:
        c.wait_send()

    def sent(s, carry):
        part_copy(s).wait_send()
        for sub in range(2):
            for way in range(2):
                ring_copy(s, way, sub).wait_send()
        return carry

    lax.fori_loop(0, Y - 1, sent, jnp.int32(0))
    part_copy(last).wait_send()
    for r in range(1, X):
        met_copy(r).wait_send()


def per_device(Z, Y, amplitudes, amplitude_mask, integrals, integral_mask, owners):
    vmem = pl.BlockSpec(memory_space=pltpu.VMEM)
    smem = pl.BlockSpec(memory_space=pltpu.SMEM)
    dma = pltpu.SemaphoreType.DMA
    steps = Z // 2
    pair = 2 * B
    return pl.pallas_call(
        functools.partial(kernel, Z, Y),
        out_shape=jax.ShapeDtypeStruct((2, 4, B, B), BF16),
        in_specs=[vmem, smem, vmem, smem, vmem],
        out_specs=vmem,
        scratch_shapes=[
            pltpu.VMEM((2 * X, C, B, B), BF16),
            pltpu.VMEM((X, UNIT, B), BF16),
            pltpu.VMEM((Z, UNIT, B), BF16),
            pltpu.VMEM((Y, 2, 2, pair, B), F32),
            pltpu.VMEM((Y, 2, 2, pair, B), BF16),
            pltpu.VMEM((Y, 2, 2, pair, B), BF16),
            pltpu.VMEM((Y, 2, 2, pair, B), BF16),
            pltpu.VMEM((Y, 2, 2, pair, B), BF16),
            pltpu.VMEM((X, pair, B), BF16),
            pltpu.VMEM((TABLE, 128), I32),
            pltpu.SMEM((TABLE, 128), I32),
            pltpu.VMEM((Z, 8, 128), I32),
            pltpu.SMEM((Z, 8, 128), I32),
            dma((4,)), dma((4,)),
            dma((6,)), dma((6,)),
            dma((2, steps)), dma((2, steps)),
            dma((Y,)), dma((Y,)),
            dma((Y - 1, 2, 2)), dma((Y - 1, 2, 2)),
            dma((X - 1,)), dma((X - 1,)),
            dma((1 + Z,)),
        ],
        compiler_params=pltpu.CompilerParams(
            collective_id=0, has_side_effects=True, vmem_limit_bytes=48 * 1024 * 1024),
        cost_estimate=pl.CostEstimate(flops=2 * 128 * 4 * B * B * B, bytes_accessed=1 << 20, transcendentals=0),
    )(amplitudes, amplitude_mask, integrals, integral_mask, owners)


def solution(mesh):
    Z, Y = mesh.shape["row"] // X, mesh.shape["col"] // 2
    return jax.shard_map(
        functools.partial(per_device, Z, Y),
        mesh=mesh,
        in_specs=(
            P("row", "col", None, None),
            P("row", "col"),
            P("row", "col", None, None),
            P("row", "col"),
            P(),
        ),
        out_specs=P("row", "col", None, None),
        check_vma=False,
    )
```

```python
import functools

import jax
import jax.numpy as jnp
from jax import lax
from jax.experimental import pallas as pl
from jax.experimental.pallas import tpu as pltpu
from jax.sharding import PartitionSpec as P


B = 128
X = 4
C = 8
V = 4
META = 16
UNIT = V * B + META
HALF = 256
F32 = jnp.float32
BF16 = jnp.bfloat16
I32 = jnp.int32


def orbit_colour(left, right, eye, row, col):
    step = jnp.dot(right.astype(BF16), left.astype(BF16), preferred_element_type=F32)
    reach = jnp.minimum(step + eye, 1.0)
    for _ in range(5):
        half = reach.astype(BF16)
        reach = jnp.minimum(jnp.dot(half, half, preferred_element_type=F32), 1.0)
    label_r = jnp.min(jnp.where(reach > 0.5, row, 999.0), axis=0, keepdims=True)
    label_c = jnp.min(jnp.where(reach > 0.5, col, 999.0), axis=1, keepdims=True)
    other_r = jnp.sum(left * label_c, axis=0, keepdims=True)
    other_c = jnp.sum(left * label_r, axis=1, keepdims=True)
    return jnp.where(label_r > other_r, 1.0, 0.0), jnp.where(label_c > other_c, 1.0, 0.0)


def flip(value):
    return value + 1.0 - 2.0 * (value - 2.0 * jnp.floor(value * 0.5))


def colours_of(owners):
    n = owners.shape[1]
    row_i = lax.broadcasted_iota(I32, (n, n), 0)
    col_i = lax.broadcasted_iota(I32, (n, n), 1)
    row, col = row_i.astype(F32), col_i.astype(F32)
    one = lambda cond: jnp.where(cond, 1.0, 0.0)
    eye = one(row_i == col_i)
    before_r, before_c = one(row_i < col_i), one(col_i < row_i)
    own_r = jnp.broadcast_to(owners, (n, n))
    own_c = jnp.sum(own_r * eye, axis=1, keepdims=True)
    same = one(own_c == own_r)
    over0 = lambda v: jnp.sum(v, axis=0, keepdims=True)
    over1 = lambda v: jnp.sum(v, axis=1, keepdims=True)
    rank_r, rank_c = over0(same * before_r), over1(same * before_c)
    count_r, count_c = over0(same), over1(same)
    even_r, even_c = one(flip(rank_r) > rank_r), one(flip(rank_c) > rank_c)
    lone_r, lone_c = even_r * one(rank_r == count_r - 1.0), even_c * one(rank_c == count_c - 1.0)
    nth_r, nth_c = over0(lone_c * before_r), over1(lone_r * before_c)
    left = one(row_i == (col_i ^ 1))
    right = same * one(rank_c == flip(rank_r)) + lone_c * lone_r * one(nth_c == flip(nth_r))
    first_r, first_c = orbit_colour(left, right, eye, row, col)
    alike = one(first_c == first_r)
    apart = 1.0 - eye
    left = one((row_i // X) == (col_i // X)) * alike * apart
    right = same * alike * apart
    lone_r, lone_c = 1.0 - over0(right), 1.0 - over1(right)
    nth_r, nth_c = over0(lone_c * alike * before_r), over1(lone_r * alike * before_c)
    right = right + lone_c * lone_r * alike * one(nth_c == flip(nth_r))
    second_r, _ = orbit_colour(left, right, eye, row, col)
    return 2.0 * first_r + second_r, rank_r


TABLE = 40


def table_of(owners, me_x, me_z, me_col, cols):
    own = owners.astype(F32)
    colour, rank = colours_of(own)
    n = owners.shape[1]

    def part(rows, make):
        at = lax.broadcasted_iota(I32, (rows, n), 0).astype(F32)
        edge = lax.broadcasted_iota(I32, (rows, n), 1)
        return jnp.sum(make(at, (edge // X).astype(F32), (edge % X).astype(F32)), axis=1, keepdims=True)

    x, z, d = me_x.astype(F32), me_z.astype(F32), me_col.astype(F32)
    slots = part(cols, lambda at, ez, ex: jnp.where((own == at) & (colour == x), ez + 1.0, 0.0))
    mine = part(8, lambda at, ez, ex: jnp.where((rank == at) & (own == d), colour + 1.0, 0.0))
    unit = part(8, lambda at, ez, ex: jnp.where((colour == x) & (ez == z), ex, 0.0))
    spare = jnp.zeros((TABLE - cols - 16, 1), F32)
    rows = jnp.concatenate([slots, mine, unit, spare], axis=0)
    return jnp.broadcast_to(rows, (TABLE, 128)).astype(I32)


LATE = ((2, 0), (1, 3))
ORDER = [(way, LATE[1 - way][k] if early else LATE[way][k])
         for early in (True, False) for k in range(2) for way in range(2)]


def kernel(
    Z, Y, amp_hbm, amp_mask, int_hbm, int_mask, owners, out,
    amp, integral, A, XI0, XI1, G, mine, part_out, part_in, ring_out, ring_in, met, table_v, table_s, meta_v, meta_s,
    xi_send, xi_recv, a_send, a_recv, z_send, z_recv, p_send, p_recv, r_send, r_recv, m_send, m_recv, local,
):
    row, col = lax.axis_index("row"), lax.axis_index("col")
    x, z, y, core = row % X, row // X, col // 2, col % 2

    int_in = pltpu.make_async_copy(int_hbm, integral, local.at[Z + 1])
    amp_in = pltpu.make_async_copy(amp_hbm, amp, local.at[Z + 2])
    int_in.start()
    amp_in.start()

    def at_x(shift):
        return (z * X + (x + shift) % X, col)

    def at_z(shift):
        return (((z + shift) % Z) * X + x, col)

    def at_y(shift):
        return (row, ((y + shift) % Y) * 2 + core)

    partner = (row, y * 2 + (1 - core))

    barrier = pltpu.get_barrier_semaphore()
    peers = [at_x(1), at_x(2), at_x(3), at_z(1), at_z(Z - 1), at_y(1), at_y(Y - 1), partner]
    for peer in peers:
        pl.semaphore_signal(barrier, inc=1, device_id=peer, device_id_type=pl.DeviceIdType.MESH)

    def copy(src, dst, send, recv, to):
        return pltpu.make_async_remote_copy(
            src_ref=src, dst_ref=dst, send_sem=send, recv_sem=recv, device_id=to,
            device_id_type=pl.DeviceIdType.MESH,
        )

    int_in.wait()
    kept = [int_mask[0, c] for c in range(C)]
    before, places = jnp.int32(0), [jnp.int32(0)] * V
    for c in range(C):
        for j in range(V):
            places[j] = jnp.where((kept[c] != 0) & (before == j), c, places[j])
        before = before + kept[c]
    XI = (XI0, XI1)
    for j in range(V):
        scale = jnp.where(before > j, 1.0, 0.0).astype(BF16)
        XI[j // 2][0, (j % 2) * B:(j % 2 + 1) * B, :] = integral[0, places[j]] * scale
    at = lax.broadcasted_iota(I32, (META, B), 0)
    meta = jnp.zeros((META, B), I32)
    for j in range(V):
        meta = jnp.where(at == j, places[j], meta)
    XI1[0, V * B - HALF:UNIT - HALF, :] = meta.astype(F32).astype(BF16)

    pl.semaphore_wait(barrier, len(peers))

    PARTS = (pl.ds(0, HALF), pl.ds(HALF, UNIT - HALF))
    xi_copies = [
        [copy(XI[h].at[0], XI[h].at[X - r], xi_send.at[h, r - 1], xi_recv.at[h, r - 1], at_x(r)) for r in (2, 1, 3)]
        for h in range(2)
    ]
    for h in range(2):
        for c in xi_copies[h]:
            c.start()

    amp_in.wait()
    for i in range(2):
        for c in range(C):
            A[i, c] = amp[i, c] * amp_mask[i, c].astype(F32).astype(BF16)
    for way in range(2):
        for r in LATE[1 - way]:
            ring_in[way, 0, r] = jnp.zeros_like(ring_in[way, 0, r])

    a_copies = [
        copy(A.at[0], A.at[6], a_send.at[0], a_recv.at[0], at_x(1)),
        copy(A.at[1], A.at[3], a_send.at[1], a_recv.at[1], at_x(3)),
        copy(A.at[1], A.at[7], a_send.at[2], a_recv.at[2], at_x(1)),
        copy(A.at[0], A.at[2], a_send.at[3], a_recv.at[3], at_x(3)),
    ]
    a_on_right = copy(A.at[6], A.at[4], a_send.at[4], a_recv.at[4], at_x(1))
    a_on_left = copy(A.at[3], A.at[5], a_send.at[5], a_recv.at[5], at_x(3))

    table_v[...] = table_of(owners[...], x, z, col, 2 * Y)
    table_copy = pltpu.make_async_copy(table_v, table_s, local.at[0])
    table_copy.start()

    far = Z // 2
    to_right = [
        [copy(G.at[(Z - s) % Z, rows], G.at[Z - 1 - s, rows], z_send.at[0, s, h], z_recv.at[0, s, h], at_z(1))
         for h, rows in enumerate(PARTS) if s < far - 1 or h == 0]
        for s in range(far)
    ]
    to_left = [
        [copy(G.at[s, rows], G.at[s + 1, rows], z_send.at[1, s, h], z_recv.at[1, s, h], at_z(Z - 1))
         for h, rows in enumerate(PARTS) if s < far - 1 or h == 1]
        for s in range(far)
    ]

    table_copy.wait()
    from_rel = (jnp.clip(table_s[2 * Y + 8, 0], 0, X - 1) - x + X) % X
    for h, rows in enumerate(PARTS):
        for c in xi_copies[h]:
            c.wait_recv()
        G[0, rows] = XI[h][from_rel]
        to_right[0][h].start()
        to_left[0][h].start()
    for c in a_copies:
        c.start()

    def meta_out(rel):
        meta_v[rel] = G[rel, V * B:UNIT, :].astype(F32).astype(I32)[0:8]
        pltpu.make_async_copy(meta_v.at[rel], meta_s.at[rel], local.at[1 + rel]).start()

    meta_out(0)
    for s in range(far - 1):
        for h in range(2):
            to_right[s][h].wait_recv()
            if s + 1 < far - 1 or h == 0:
                to_right[s + 1][h].start()
            to_left[s][h].wait_recv()
            if s + 1 < far - 1:
                to_left[s + 1][h].start()
            elif h == 1:
                to_left[s + 1][0].start()
        meta_out(Z - 1 - s)
        meta_out(s + 1)
        if s == 2:
            a_copies[0].wait_recv()
            a_on_right.start()
            a_copies[1].wait_recv()
            a_on_left.start()
    to_right[far - 1][0].wait_recv()
    to_left[far - 1][0].wait_recv()
    meta_out(far)
    a_copies[2].wait_recv()
    a_copies[3].wait_recv()
    a_on_right.wait_recv()
    a_on_left.wait_recv()
    for rel in range(Z):
        pltpu.make_async_copy(meta_v.at[rel], meta_s.at[rel], local.at[1 + rel]).wait()

    far_y = Y // 2

    def part_copy(n):
        return copy(part_out.at[n], part_in.at[n], p_send.at[n], p_recv.at[n], partner)

    def ring_copy(s, way, r):
        return copy(
            ring_out.at[way, s, r], ring_in.at[way, s, r], r_send.at[way, s, r], r_recv.at[way, s, r],
            at_y(1 if way == 0 else Y - 1),
        )

    def products(n, slot_y):
        for whose in (1, 0):
            owner = slot_y * 2 + (core + whose) % 2
            named = table_s[owner, 0]
            filled = jnp.where(named > 0, 1.0, 0.0).astype(F32)
            rel = jnp.clip(named - 1, 0, Z - 1) - z
            rel = jnp.where(rel < 0, rel + Z, rel)
            where = [jnp.clip(meta_s[rel, j, 0], 0, C - 1) for j in range(V)]
            unit = G[rel, 0:V * B, :]
            wide = jnp.concatenate([unit[j * B:(j + 1) * B] for j in range(V)], axis=1)
            for r in range(X):
                tiles = jnp.concatenate([A[2 * r:2 * r + 2, where[j]].reshape(2 * B, B) for j in range(V)], axis=1)
                total = filled * lax.dot_general(tiles, wide, (((1,), (1,)), ((), ())), preferred_element_type=F32)
                if whose == 0:
                    mine[n, r] = total
                else:
                    part_out[n, r] = total.astype(BF16)
            if whose == 1:
                part_copy(n).start()

    def one(way, s):
        products(2 * s + way, (y + (far_y - s if way == 0 else far_y + s)) % Y)

    products(0, (y + far_y) % Y)
    one(0, 1)
    part_copy(0).wait_recv()
    for k in range(2):
        for way in range(2):
            r = LATE[way][k]
            ring_out[way, 0, r] = (mine[0, r] + part_in[0, r].astype(F32)).astype(BF16)
            ring_copy(0, way, r).start()
    one(1, 1)

    def ring_step(s, carry):
        part_copy(2 * s).wait_recv()
        part_copy(2 * s + 1).wait_recv()
        for way, r in ORDER:
            if r in LATE[way]:
                ring_copy(s - 1, way, r).wait_recv()
            else:
                @pl.when(s > 1)
                def _():
                    ring_copy(s - 1, way, r).wait_recv()
            n = 2 * s + way
            total = mine[n, r] + part_in[n, r].astype(F32) + ring_in[way, s - 1, r].astype(F32)
            ring_out[way, s, r] = total.astype(BF16)
            ring_copy(s, way, r).start()

        @pl.when(s < far_y - 1)
        def _():
            one(0, s + 1)
            one(1, s + 1)
        return carry

    lax.fori_loop(1, far_y, ring_step, jnp.int32(0))
    products(1, y)

    def met_copy(r):
        return copy(ring_out.at[0, far_y, r], met.at[X - r], m_send.at[r - 1], m_recv.at[r - 1], at_x(r))

    last = far_y - 1
    part_copy(1).wait_recv()
    for way, r in ORDER:
        ring_copy(last, way, r).wait_recv()
        if r in LATE[way]:
            total = (mine[1, r] + part_in[1, r].astype(F32)) + (
                ring_in[0, last, r].astype(F32) + ring_in[1, last, r].astype(F32))
            if r == 0:
                met[0] = total.astype(BF16)
            else:
                ring_out[0, far_y, r] = total.astype(BF16)
                met_copy(r).start()
    for r in range(1, X):
        met_copy(r).wait_recv()
    slots = out.shape[1]
    for t in range(slots):
        named = table_s[2 * Y + t, 0]
        filled = jnp.where(named > 0, 1.0, 0.0).astype(BF16)
        rel = jnp.clip(named - 1, 0, X - 1) - x
        tiles = met[jnp.where(rel < 0, rel + X, rel)] * filled
        for i in range(2):
            out[i, t] = tiles[i * B:(i + 1) * B]

    for c in [*xi_copies[0], *xi_copies[1], *a_copies, a_on_right, a_on_left]:
        c.wait_send()
    for s in range(far):
        for c in to_right[s] + to_left[s]:
            c.wait_send()
    for n in range(Y):
        part_copy(n).wait_send()
    for s in range(far_y):
        for way, r in ORDER:
            if s > 0 or r in LATE[way]:
                ring_copy(s, way, r).wait_send()
    for r in range(1, X):
        met_copy(r).wait_send()


def per_device(Z, Y, amplitudes, amplitude_mask, integrals, integral_mask, owners):
    vmem = pl.BlockSpec(memory_space=pltpu.VMEM)
    smem = pl.BlockSpec(memory_space=pltpu.SMEM)
    hbm = pl.BlockSpec(memory_space=pl.ANY)
    dma = pltpu.SemaphoreType.DMA
    far, far_y = Z // 2, Y // 2
    piece = 2 * B
    return pl.pallas_call(
        functools.partial(kernel, Z, Y),
        out_shape=jax.ShapeDtypeStruct((2, 4, B, B), BF16),
        in_specs=[hbm, smem, hbm, smem, vmem],
        out_specs=vmem,
        scratch_shapes=[
            pltpu.VMEM((2, C, B, B), BF16),
            pltpu.VMEM((1, C, B, B), BF16),
            pltpu.VMEM((2 * X, C, B, B), BF16),
            pltpu.VMEM((X, HALF, B), BF16),
            pltpu.VMEM((X, UNIT - HALF, B), BF16),
            pltpu.VMEM((Z, UNIT, B), BF16),
            pltpu.VMEM((Y, X, piece, B), F32),
            pltpu.VMEM((Y, X, piece, B), BF16),
            pltpu.VMEM((Y, X, piece, B), BF16),
            pltpu.VMEM((2, far_y + 1, X, piece, B), BF16),
            pltpu.VMEM((2, far_y, X, piece, B), BF16),
            pltpu.VMEM((X, piece, B), BF16),
            pltpu.VMEM((TABLE, 128), I32),
            pltpu.SMEM((TABLE, 128), I32),
            pltpu.VMEM((Z, 8, 128), I32),
            pltpu.SMEM((Z, 8, 128), I32),
            dma((2, X - 1)), dma((2, X - 1)),
            dma((6,)), dma((6,)),
            dma((2, far, 2)), dma((2, far, 2)),
            dma((Y,)), dma((Y,)),
            dma((2, far_y, X)), dma((2, far_y, X)),
            dma((X - 1,)), dma((X - 1,)),
            dma((3 + Z,)),
        ],
        compiler_params=pltpu.CompilerParams(
            collective_id=0, has_side_effects=True, vmem_limit_bytes=56 * 1024 * 1024),
        cost_estimate=pl.CostEstimate(flops=2 * 128 * 4 * B * B * B, bytes_accessed=1 << 20, transcendentals=0),
    )(amplitudes, amplitude_mask, integrals, integral_mask, owners.reshape(1, -1))


def solution(mesh):
    Z, Y = mesh.shape["row"] // X, mesh.shape["col"] // 2
    return jax.shard_map(
        functools.partial(per_device, Z, Y),
        mesh=mesh,
        in_specs=(
            P("row", "col", None, None),
            P("row", "col"),
            P("row", "col", None, None),
            P("row", "col"),
            P(),
        ),
        out_specs=P("row", "col", None, None),
        check_vma=False,
    )
```

```python
import functools

import jax
import jax.numpy as jnp
from jax import lax
from jax.experimental import pallas as pl
from jax.experimental.pallas import tpu as pltpu
from jax.sharding import PartitionSpec as P


B = 128
X = 4
C = 8
V = 4
META = 16
UNIT = V * B + META
HALF = 256
F32 = jnp.float32
BF16 = jnp.bfloat16
I32 = jnp.int32


def orbit_colour(left, right, eye, row, col):
    step = jnp.dot(right.astype(BF16), left.astype(BF16), preferred_element_type=F32)
    reach = jnp.minimum(step + eye, 1.0)
    for _ in range(5):
        half = reach.astype(BF16)
        reach = jnp.minimum(jnp.dot(half, half, preferred_element_type=F32), 1.0)
    label_r = jnp.min(jnp.where(reach > 0.5, row, 999.0), axis=0, keepdims=True)
    label_c = jnp.min(jnp.where(reach > 0.5, col, 999.0), axis=1, keepdims=True)
    other_r = jnp.sum(left * label_c, axis=0, keepdims=True)
    other_c = jnp.sum(left * label_r, axis=1, keepdims=True)
    return jnp.where(label_r > other_r, 1.0, 0.0), jnp.where(label_c > other_c, 1.0, 0.0)


def flip(value):
    return value + 1.0 - 2.0 * (value - 2.0 * jnp.floor(value * 0.5))


def colours_of(owners):
    n = owners.shape[1]
    row_i = lax.broadcasted_iota(I32, (n, n), 0)
    col_i = lax.broadcasted_iota(I32, (n, n), 1)
    row, col = row_i.astype(F32), col_i.astype(F32)
    one = lambda cond: jnp.where(cond, 1.0, 0.0)
    eye = one(row_i == col_i)
    before_r, before_c = one(row_i < col_i), one(col_i < row_i)
    own_r = jnp.broadcast_to(owners, (n, n))
    own_c = jnp.sum(own_r * eye, axis=1, keepdims=True)
    same = one(own_c == own_r)
    over0 = lambda v: jnp.sum(v, axis=0, keepdims=True)
    over1 = lambda v: jnp.sum(v, axis=1, keepdims=True)
    rank_r, rank_c = over0(same * before_r), over1(same * before_c)
    count_r, count_c = over0(same), over1(same)
    even_r, even_c = one(flip(rank_r) > rank_r), one(flip(rank_c) > rank_c)
    lone_r, lone_c = even_r * one(rank_r == count_r - 1.0), even_c * one(rank_c == count_c - 1.0)
    nth_r, nth_c = over0(lone_c * before_r), over1(lone_r * before_c)
    left = one(row_i == (col_i ^ 1))
    right = same * one(rank_c == flip(rank_r)) + lone_c * lone_r * one(nth_c == flip(nth_r))
    first_r, first_c = orbit_colour(left, right, eye, row, col)
    alike = one(first_c == first_r)
    apart = 1.0 - eye
    left = one((row_i // X) == (col_i // X)) * alike * apart
    right = same * alike * apart
    lone_r, lone_c = 1.0 - over0(right), 1.0 - over1(right)
    nth_r, nth_c = over0(lone_c * alike * before_r), over1(lone_r * alike * before_c)
    right = right + lone_c * lone_r * alike * one(nth_c == flip(nth_r))
    second_r, _ = orbit_colour(left, right, eye, row, col)
    return 2.0 * first_r + second_r, rank_r


TABLE = 40


def table_of(owners, me_x, me_z, me_col, cols):
    own = owners.astype(F32)
    colour, rank = colours_of(own)
    n = owners.shape[1]

    def part(rows, make):
        at = lax.broadcasted_iota(I32, (rows, n), 0).astype(F32)
        edge = lax.broadcasted_iota(I32, (rows, n), 1)
        return jnp.sum(make(at, (edge // X).astype(F32), (edge % X).astype(F32)), axis=1, keepdims=True)

    x, z, d = me_x.astype(F32), me_z.astype(F32), me_col.astype(F32)
    slots = part(cols, lambda at, ez, ex: jnp.where((own == at) & (colour == x), ez + 1.0, 0.0))
    mine = part(8, lambda at, ez, ex: jnp.where((rank == at) & (own == d), colour + 1.0, 0.0))
    unit = part(8, lambda at, ez, ex: jnp.where((colour == x) & (ez == z), ex, 0.0))
    spare = jnp.zeros((TABLE - cols - 16, 1), F32)
    rows = jnp.concatenate([slots, mine, unit, spare], axis=0)
    return jnp.broadcast_to(rows, (TABLE, 128)).astype(I32)


LATE = ((2, 0), (1, 3))
ORDER = [(way, LATE[1 - way][k] if early else LATE[way][k])
         for early in (True, False) for k in range(2) for way in range(2)]


def kernel(
    Z, Y, amp_hbm, amp_mask, int_hbm, int_mask, owners, out,
    amp, integral, A0, A1, A2, A3, XI0, XI1, G, partial, part_out, part_in, ring_out, ring_in, own_out, met, table_v, table_s, meta_v, meta_s,
    xi_send, xi_recv, a_send, a_recv, z_send, z_recv, p_send, p_recv, r_send, r_recv, m_send, m_recv, local,
):
    row, col = lax.axis_index("row"), lax.axis_index("col")
    x, z, y, core = row % X, row // X, col // 2, col % 2

    int_in = pltpu.make_async_copy(int_hbm, integral, local.at[Z + 1])
    amp_in = pltpu.make_async_copy(amp_hbm, amp, local.at[Z + 2])
    int_in.start()
    amp_in.start()

    def at_x(shift):
        return (z * X + (x + shift) % X, col)

    def at_z(shift):
        return (((z + shift) % Z) * X + x, col)

    def at_y(shift):
        return (row, ((y + shift) % Y) * 2 + core)

    def at_xy(right, up):
        return (z * X + (x + right) % X, ((y + up) % Y) * 2 + core)

    partner = (row, y * 2 + (1 - core))

    barrier = pltpu.get_barrier_semaphore()
    peers = [at_x(1), at_x(2), at_x(3), at_z(1), at_z(Z - 1), at_y(1), at_y(Y - 1), partner]
    peers += [at_xy(r, up) for r in range(1, X) for up in (1, Y - 1)]
    for peer in peers:
        pl.semaphore_signal(barrier, inc=1, device_id=peer, device_id_type=pl.DeviceIdType.MESH)

    def copy(src, dst, send, recv, to):
        return pltpu.make_async_remote_copy(
            src_ref=src, dst_ref=dst, send_sem=send, recv_sem=recv, device_id=to,
            device_id_type=pl.DeviceIdType.MESH,
        )

    int_in.wait()
    kept = [int_mask[0, c] for c in range(C)]
    before, places = jnp.int32(0), [jnp.int32(0)] * V
    for c in range(C):
        for j in range(V):
            places[j] = jnp.where((kept[c] != 0) & (before == j), c, places[j])
        before = before + kept[c]
    XI = (XI0, XI1)
    for j in range(V):
        scale = jnp.where(before > j, 1.0, 0.0).astype(BF16)
        XI[j // 2][0, (j % 2) * B:(j % 2 + 1) * B, :] = integral[0, places[j]] * scale
    at = lax.broadcasted_iota(I32, (META, B), 0)
    meta = jnp.zeros((META, B), I32)
    for j in range(V):
        meta = jnp.where(at == j, places[j], meta)
    XI1[0, V * B - HALF:UNIT - HALF, :] = meta.astype(F32).astype(BF16)

    pl.semaphore_wait(barrier, len(peers))

    PARTS = (pl.ds(0, HALF), pl.ds(HALF, UNIT - HALF))
    xi_copies = [
        [copy(XI[h].at[0], XI[h].at[X - r], xi_send.at[h, r - 1], xi_recv.at[h, r - 1], at_x(r)) for r in (2, 1, 3)]
        for h in range(2)
    ]
    for h in range(2):
        for c in xi_copies[h]:
            c.start()

    amp_in.wait()
    for i in range(2):
        for c in range(C):
            A0[i, c] = amp[i, c] * amp_mask[i, c].astype(F32).astype(BF16)
    for way in range(2):
        for r in LATE[1 - way]:
            ring_in[way, 0, r] = jnp.zeros_like(ring_in[way, 0, r])

    A = (A0, A1, A2, A3)
    a_copies = [
        copy(A0.at[0], A3.at[0], a_send.at[0], a_recv.at[0], at_x(1)),
        copy(A0.at[1], A1.at[1], a_send.at[1], a_recv.at[1], at_x(3)),
        copy(A0.at[1], A3.at[1], a_send.at[2], a_recv.at[2], at_x(1)),
        copy(A0.at[0], A1.at[0], a_send.at[3], a_recv.at[3], at_x(3)),
    ]
    a_on_right = copy(A3.at[0], A2.at[0], a_send.at[4], a_recv.at[4], at_x(1))
    a_on_left = copy(A1.at[1], A2.at[1], a_send.at[5], a_recv.at[5], at_x(3))

    table_v[...] = table_of(owners[...], x, z, col, 2 * Y)
    table_copy = pltpu.make_async_copy(table_v, table_s, local.at[0])
    table_copy.start()

    far = Z // 2
    to_right = [
        [copy(G.at[(Z - s) % Z, rows], G.at[Z - 1 - s, rows], z_send.at[0, s, h], z_recv.at[0, s, h], at_z(1))
         for h, rows in enumerate(PARTS) if s < far - 1 or h == 0]
        for s in range(far)
    ]
    to_left = [
        [copy(G.at[s, rows], G.at[s + 1, rows], z_send.at[1, s, h], z_recv.at[1, s, h], at_z(Z - 1))
         for h, rows in enumerate(PARTS) if s < far - 1 or h == 1]
        for s in range(far)
    ]

    table_copy.wait()
    from_rel = (jnp.clip(table_s[2 * Y + 8, 0], 0, X - 1) - x + X) % X
    for h, rows in enumerate(PARTS):
        for c in xi_copies[h]:
            c.wait_recv()
        G[0, rows] = XI[h][from_rel]
        to_right[0][h].start()
        to_left[0][h].start()
    for c in a_copies:
        c.start()

    def meta_copy(rel):
        return pltpu.make_async_copy(meta_v.at[rel], meta_s.at[rel], local.at[1 + rel])

    def meta_out(rel):
        meta_v[rel] = G[rel, V * B:UNIT, :].astype(F32).astype(I32)[0:8]
        meta_copy(rel).start()

    def products(rel, pieces):
        where = [jnp.clip(meta_s[rel, j, 0], 0, C - 1) for j in range(V)]
        wide = jnp.concatenate([G[rel, j * B:(j + 1) * B, :] for j in range(V)], axis=1)
        for r in pieces:
            tiles = jnp.concatenate([A[r][:, where[j]].reshape(2 * B, B) for j in range(V)], axis=1)
            total = lax.dot_general(tiles, wide, (((1,), (1,)), ((), ())), preferred_element_type=F32)
            partial[rel, r] = total.astype(BF16)

    meta_out(0)
    seen, crossed = [0], []
    for s in range(far - 1):
        for h in range(2):
            to_right[s][h].wait_recv()
            if s + 1 < far - 1 or h == 0:
                to_right[s + 1][h].start()
            to_left[s][h].wait_recv()
            if s + 1 < far - 1:
                to_left[s + 1][h].start()
            elif h == 1:
                to_left[s + 1][0].start()
        meta_out(Z - 1 - s)
        meta_out(s + 1)
        if s == far - 4:
            a_copies[0].wait_recv()
            a_on_right.start()
            a_copies[1].wait_recv()
            a_on_left.start()
        if s == far - 3:
            a_copies[2].wait_recv()
            a_copies[3].wait_recv()
        now = [0] if s == 0 else [Z - s, s]
        for rel in now:
            meta_copy(rel).wait()
            products(rel, (0,))
        if s >= far - 3:
            for rel in [rel for rel in seen if rel not in crossed]:
                products(rel, (1, 3))
                crossed.append(rel)
        seen += [Z - 1 - s, s + 1]
    for rel in seen[-2:]:
        meta_copy(rel).wait()
        products(rel, (0,))
    for rel in [rel for rel in seen if rel not in crossed]:
        products(rel, (1, 3))
    a_on_right.wait_recv()
    a_on_left.wait_recv()
    for rel in seen:
        products(rel, (2,))
    to_right[far - 1][0].wait_recv()
    to_left[far - 1][0].wait_recv()
    meta_out(far)
    meta_copy(far).wait()
    products(far, range(X))

    far_y = Y // 2

    def part_copy(n):
        return copy(part_out.at[n], part_in.at[n], p_send.at[n], p_recv.at[n], partner)

    def ring_copy(s, way, r):
        return copy(
            ring_out.at[way, s, r], ring_in.at[way, s, r], r_send.at[way, s, r], r_recv.at[way, s, r],
            at_y(1 if way == 0 else Y - 1),
        )

    def slot_of(n):
        if isinstance(n, int) and n < 2:
            return (y + far_y) % Y if n == 0 else y
        s, way = n // 2, n % 2
        return (y + far_y + (2 * way - 1) * s + Y) % Y

    def source_of(n, whose):
        named = table_s[slot_of(n) * 2 + (core + whose) % 2, 0]
        rel = jnp.clip(named - 1, 0, Z - 1) - z
        return jnp.where(rel < 0, rel + Z, rel), jnp.where(named > 0, 1.0, 0.0).astype(F32)

    def stage(n):
        rel, filled = source_of(n, 1)
        part_out[n] = partial[rel] * filled.astype(BF16)
        part_copy(n).start()

    stage(0)
    stage(2)
    stage(3)
    rel_0, filled_0 = source_of(0, 0)
    part_copy(0).wait_recv()
    for k in range(2):
        for way in range(2):
            r = LATE[way][k]
            ring_out[way, 0, r] = (partial[rel_0, r].astype(F32) * filled_0 + part_in[0, r].astype(F32)).astype(BF16)
            ring_copy(0, way, r).start()
    for n in (*range(4, Y), 1):
        stage(n)

    def last_copy(way, r):
        if way == 2:
            source, to = own_out.at[r], at_x(r)
        else:
            source, to = ring_out.at[way, far_y - 1, r], at_xy(r, 1 if way == 0 else Y - 1)
        return copy(source, met.at[way, (X - r) % X], m_send.at[way, r], m_recv.at[way, r], to)

    def ring_sums(s, way, r, source):
        rel, filled = source
        own = partial[rel, r].astype(F32) * filled
        return (own + part_in[2 * s + way, r].astype(F32) + ring_in[way, s - 1, r].astype(F32)).astype(BF16)

    def ring_step(s, carry):
        part_copy(2 * s).wait_recv()
        part_copy(2 * s + 1).wait_recv()
        sources = [source_of(2 * s + way, 0) for way in range(2)]
        for way, r in ORDER:
            if r in LATE[way]:
                ring_copy(s - 1, way, r).wait_recv()
            else:
                @pl.when(s > 1)
                def _():
                    ring_copy(s - 1, way, r).wait_recv()
            ring_out[way, s, r] = ring_sums(s, way, r, sources[way])
            ring_copy(s, way, r).start()
        return carry

    last = far_y - 1
    lax.fori_loop(1, last, ring_step, jnp.int32(0))
    part_copy(1).wait_recv()
    rel_1, filled_1 = source_of(1, 0)
    for r in (2, 1, 3, 0):
        sums = (partial[rel_1, r].astype(F32) * filled_1 + part_in[1, r].astype(F32)).astype(BF16)
        if r == 0:
            met[2, 0] = sums
        else:
            own_out[r] = sums
            last_copy(2, r).start()
    part_copy(2 * last).wait_recv()
    part_copy(2 * last + 1).wait_recv()
    sources = [source_of(2 * last + way, 0) for way in range(2)]
    for way, r in ORDER:
        ring_copy(last - 1, way, r).wait_recv()
        ring_out[way, last, r] = ring_sums(last, way, r, sources[way])
        last_copy(way, r).start()

    for c in [*xi_copies[0], *xi_copies[1], *a_copies, a_on_right, a_on_left]:
        c.wait_send()
    for s in range(far):
        for c in to_right[s] + to_left[s]:
            c.wait_send()
    for n in range(Y):
        part_copy(n).wait_send()
    for s in range(last):
        for way, r in ORDER:
            if s > 0 or r in LATE[way]:
                ring_copy(s, way, r).wait_send()

    for r in range(1, X):
        last_copy(2, r).wait_recv()
    for way, r in ORDER:
        last_copy(way, r).wait_recv()
    slots = out.shape[1]
    for t in range(slots):
        named = table_s[2 * Y + t, 0]
        filled = jnp.where(named > 0, 1.0, 0.0).astype(F32)
        rel = jnp.clip(named - 1, 0, X - 1) - x
        rel = jnp.where(rel < 0, rel + X, rel)
        tiles = (filled * (met[0, rel].astype(F32) + met[1, rel].astype(F32) + met[2, rel].astype(F32))).astype(BF16)
        for i in range(2):
            out[i, t] = tiles[i * B:(i + 1) * B]

    for r in range(1, X):
        last_copy(2, r).wait_send()
    for way, r in ORDER:
        last_copy(way, r).wait_send()


def per_device(Z, Y, amplitudes, amplitude_mask, integrals, integral_mask, owners):
    vmem = pl.BlockSpec(memory_space=pltpu.VMEM)
    smem = pl.BlockSpec(memory_space=pltpu.SMEM)
    hbm = pl.BlockSpec(memory_space=pl.ANY)
    dma = pltpu.SemaphoreType.DMA
    far, far_y = Z // 2, Y // 2
    piece = 2 * B
    return pl.pallas_call(
        functools.partial(kernel, Z, Y),
        out_shape=jax.ShapeDtypeStruct((2, 4, B, B), BF16),
        in_specs=[hbm, smem, hbm, smem, vmem],
        out_specs=vmem,
        scratch_shapes=[
            pltpu.VMEM((2, C, B, B), BF16),
            pltpu.VMEM((1, C, B, B), BF16),
            *[pltpu.VMEM((2, C, B, B), BF16)] * X,
            pltpu.VMEM((X, HALF, B), BF16),
            pltpu.VMEM((X, UNIT - HALF, B), BF16),
            pltpu.VMEM((Z, UNIT, B), BF16),
            pltpu.VMEM((Z, X, piece, B), BF16),
            pltpu.VMEM((Y, X, piece, B), BF16),
            pltpu.VMEM((Y, X, piece, B), BF16),
            pltpu.VMEM((2, far_y, X, piece, B), BF16),
            pltpu.VMEM((2, far_y - 1, X, piece, B), BF16),
            pltpu.VMEM((X, piece, B), BF16),
            pltpu.VMEM((3, X, piece, B), BF16),
            pltpu.VMEM((TABLE, 128), I32),
            pltpu.SMEM((TABLE, 128), I32),
            pltpu.VMEM((Z, 8, 128), I32),
            pltpu.SMEM((Z, 8, 128), I32),
            dma((2, X - 1)), dma((2, X - 1)),
            dma((6,)), dma((6,)),
            dma((2, far, 2)), dma((2, far, 2)),
            dma((Y,)), dma((Y,)),
            dma((2, far_y - 1, X)), dma((2, far_y - 1, X)),
            dma((3, X)), dma((3, X)),
            dma((3 + Z,)),
        ],
        compiler_params=pltpu.CompilerParams(
            collective_id=0, has_side_effects=True, vmem_limit_bytes=56 * 1024 * 1024),
        cost_estimate=pl.CostEstimate(flops=2 * 128 * 4 * B * B * B, bytes_accessed=1 << 20, transcendentals=0),
    )(amplitudes, amplitude_mask, integrals, integral_mask, owners.reshape(1, -1))


def solution(mesh):
    Z, Y = mesh.shape["row"] // X, mesh.shape["col"] // 2
    return jax.shard_map(
        functools.partial(per_device, Z, Y),
        mesh=mesh,
        in_specs=(
            P("row", "col", None, None),
            P("row", "col"),
            P("row", "col", None, None),
            P("row", "col"),
            P(),
        ),
        out_specs=P("row", "col", None, None),
        check_vma=False,
    )
```

```python
import functools

import jax
import jax.numpy as jnp
from jax import lax
from jax.experimental import pallas as pl
from jax.experimental.pallas import tpu as pltpu
from jax.sharding import PartitionSpec as P


B = 128
X = 4
C = 8
V = 4
META = 16
UNIT = V * B + META
PARTS = [(0, META + B)] + [(META + j * B, B) for j in range(1, V)]
F32 = jnp.float32
BF16 = jnp.bfloat16
I32 = jnp.int32


def orbit_colour(left, right, eye, row, col):
    step = jnp.dot(right.astype(BF16), left.astype(BF16), preferred_element_type=F32)
    reach = jnp.minimum(step + eye, 1.0)
    for _ in range(5):
        half = reach.astype(BF16)
        reach = jnp.minimum(jnp.dot(half, half, preferred_element_type=F32), 1.0)
    label_r = jnp.min(jnp.where(reach > 0.5, row, 999.0), axis=0, keepdims=True)
    label_c = jnp.min(jnp.where(reach > 0.5, col, 999.0), axis=1, keepdims=True)
    other_r = jnp.sum(left * label_c, axis=0, keepdims=True)
    other_c = jnp.sum(left * label_r, axis=1, keepdims=True)
    return jnp.where(label_r > other_r, 1.0, 0.0), jnp.where(label_c > other_c, 1.0, 0.0)


def flip(value):
    return value + 1.0 - 2.0 * (value - 2.0 * jnp.floor(value * 0.5))


def colours_of(owners):
    n = owners.shape[1]
    row_i = lax.broadcasted_iota(I32, (n, n), 0)
    col_i = lax.broadcasted_iota(I32, (n, n), 1)
    row, col = row_i.astype(F32), col_i.astype(F32)
    one = lambda cond: jnp.where(cond, 1.0, 0.0)
    eye = one(row_i == col_i)
    before_r, before_c = one(row_i < col_i), one(col_i < row_i)
    own_r = jnp.broadcast_to(owners, (n, n))
    own_c = jnp.sum(own_r * eye, axis=1, keepdims=True)
    same = one(own_c == own_r)
    over0 = lambda v: jnp.sum(v, axis=0, keepdims=True)
    over1 = lambda v: jnp.sum(v, axis=1, keepdims=True)
    rank_r, rank_c = over0(same * before_r), over1(same * before_c)
    count_r, count_c = over0(same), over1(same)
    even_r, even_c = one(flip(rank_r) > rank_r), one(flip(rank_c) > rank_c)
    lone_r, lone_c = even_r * one(rank_r == count_r - 1.0), even_c * one(rank_c == count_c - 1.0)
    nth_r, nth_c = over0(lone_c * before_r), over1(lone_r * before_c)
    left = one(row_i == (col_i ^ 1))
    right = same * one(rank_c == flip(rank_r)) + lone_c * lone_r * one(nth_c == flip(nth_r))
    first_r, first_c = orbit_colour(left, right, eye, row, col)
    alike = one(first_c == first_r)
    apart = 1.0 - eye
    left = one((row_i // X) == (col_i // X)) * alike * apart
    right = same * alike * apart
    lone_r, lone_c = 1.0 - over0(right), 1.0 - over1(right)
    nth_r, nth_c = over0(lone_c * alike * before_r), over1(lone_r * alike * before_c)
    right = right + lone_c * lone_r * alike * one(nth_c == flip(nth_r))
    second_r, _ = orbit_colour(left, right, eye, row, col)
    return 2.0 * first_r + second_r, rank_r


TABLE = 40


def table_of(owners, me_x, me_z, me_col, cols):
    own = owners.astype(F32)
    colour, rank = colours_of(own)
    n = owners.shape[1]

    def part(rows, make):
        at = lax.broadcasted_iota(I32, (rows, n), 0).astype(F32)
        edge = lax.broadcasted_iota(I32, (rows, n), 1)
        return jnp.sum(make(at, (edge // X).astype(F32), (edge % X).astype(F32)), axis=1, keepdims=True)

    x, z, d = me_x.astype(F32), me_z.astype(F32), me_col.astype(F32)
    slots = part(cols, lambda at, ez, ex: jnp.where((own == at) & (colour == x), ez + 1.0, 0.0))
    mine = part(8, lambda at, ez, ex: jnp.where((rank == at) & (own == d), colour + 1.0, 0.0))
    unit = part(8, lambda at, ez, ex: jnp.where((colour == x) & (ez == z), ex, 0.0))
    spare = jnp.zeros((TABLE - cols - 16, 1), F32)
    rows = jnp.concatenate([slots, mine, unit, spare], axis=0)
    return jnp.broadcast_to(rows, (TABLE, 128)).astype(I32)


LATE = ((2, 0), (1, 3))
ORDER = [(way, LATE[1 - way][k] if early else LATE[way][k])
         for early in (True, False) for k in range(2) for way in range(2)]


def kernel(
    Z, Y, amp_hbm, amp_mask, int_hbm, int_mask, owners, out,
    amp, integral, A0, A1, A2, A3, XI0, XI1, XI2, XI3, G, partial, part_out, part_in, ring_out, ring_in, own_out, met, table_v, table_s, meta_v, meta_s,
    xi_send, xi_recv, a_send, a_recv, z_send, z_recv, f_send, f_recv, p_send, p_recv, r_send, r_recv, m_send, m_recv, local,
):
    row, col = lax.axis_index("row"), lax.axis_index("col")
    x, z, y, core = row % X, row // X, col // 2, col % 2

    def at_x(shift):
        return (z * X + (x + shift) % X, col)

    def at_z(shift):
        return (((z + shift) % Z) * X + x, col)

    def at_y(shift):
        return (row, ((y + shift) % Y) * 2 + core)

    def at_xy(right, up):
        return (z * X + (x + right) % X, ((y + up) % Y) * 2 + core)

    partner = (row, y * 2 + (1 - core))

    barrier = pltpu.get_barrier_semaphore()
    peers = [at_x(1), at_x(2), at_x(3), at_z(1), at_z(Z - 1), at_y(1), at_y(Y - 1), partner]
    peers += [at_xy(r, up) for r in range(1, X) for up in (1, Y - 1)]
    for peer in peers:
        pl.semaphore_signal(barrier, inc=1, device_id=peer, device_id_type=pl.DeviceIdType.MESH)

    int_in = pltpu.make_async_copy(int_hbm, integral, local.at[Z + 1])
    amp_in = pltpu.make_async_copy(amp_hbm, amp, local.at[Z + 2])
    int_in.start()
    amp_in.start()

    def copy(src, dst, send, recv, to):
        return pltpu.make_async_remote_copy(
            src_ref=src, dst_ref=dst, send_sem=send, recv_sem=recv, device_id=to,
            device_id_type=pl.DeviceIdType.MESH,
        )

    int_in.wait()
    kept = [int_mask[0, c] for c in range(C)]
    before, places = jnp.int32(0), [jnp.int32(0)] * V
    for c in range(C):
        for j in range(V):
            places[j] = jnp.where((kept[c] != 0) & (before == j), c, places[j])
        before = before + kept[c]
    XI = (XI0, XI1, XI2, XI3)
    at = lax.broadcasted_iota(I32, (META, B), 0)
    meta = jnp.zeros((META, B), I32)
    for j in range(V):
        meta = jnp.where(at == j, places[j], meta)
    XI0[0, 0:META] = meta.astype(F32).astype(BF16)
    for j in range(V):
        scale = jnp.where(before > j, 1.0, 0.0).astype(BF16)
        first = META if j == 0 else 0
        XI[j][0, first:first + B] = integral[0, places[j]] * scale

    pl.semaphore_wait(barrier, len(peers))

    xi_copies = [
        [copy(XI[h].at[0], XI[h].at[X - r], xi_send.at[h], xi_recv.at[h], at_x(r)) for r in (2, 1, 3)]
        for h in range(V)
    ]

    def xi_all(h):
        return copy(XI[h].at[1:X], XI[h].at[1:X], xi_send.at[h], xi_recv.at[h], at_x(1))

    for h in range(V):
        for c in xi_copies[h]:
            c.start()

    amp_in.wait()
    for i in range(2):
        for c in range(C):
            A0[i, c] = amp[i, c] * amp_mask[i, c].astype(F32).astype(BF16)

    A = (A0, A1, A2, A3)
    a_copies = [
        copy(A0.at[0], A3.at[0], a_send.at[0], a_recv.at[0], at_x(1)),
        copy(A0.at[1], A1.at[1], a_send.at[0], a_recv.at[1], at_x(3)),
        copy(A0.at[1], A3.at[1], a_send.at[1], a_recv.at[2], at_x(1)),
        copy(A0.at[0], A1.at[0], a_send.at[1], a_recv.at[3], at_x(3)),
    ]
    a_on_right = copy(A3.at[0], A2.at[0], a_send.at[2], a_recv.at[4], at_x(1))
    a_on_left = copy(A1.at[1], A2.at[1], a_send.at[2], a_recv.at[5], at_x(3))

    table_v[...] = table_of(owners[...], x, z, col, 2 * Y)
    table_copy = pltpu.make_async_copy(table_v, table_s, local.at[0])
    table_copy.start()

    far = Z // 2
    RIGHT, LEFT = range(0, V // 2), range(V // 2, V)

    def rows_of(h):
        return pl.ds(*PARTS[h])

    to_right = [
        {h: copy(G.at[(Z - s) % Z, rows_of(h)], G.at[Z - 1 - s, rows_of(h)], z_send.at[0, s // (far - 1)], z_recv.at[0, s, h], at_z(1))
         for h in (range(V) if s < far - 1 else RIGHT)}
        for s in range(far)
    ]
    to_left = [
        {h: copy(G.at[s, rows_of(h)], G.at[s + 1, rows_of(h)], z_send.at[1, s // (far - 1)], z_recv.at[1, s, h], at_z(Z - 1))
         for h in (range(V) if s < far - 1 else LEFT)}
        for s in range(far)
    ]

    table_copy.wait()
    from_rel = (jnp.clip(table_s[2 * Y + 8, 0], 0, X - 1) - x + X) % X
    for h in range(V):
        xi_all(h).wait_recv()
        G[0, rows_of(h)] = XI[h][from_rel]
        to_right[0][h].start()
        to_left[0][h].start()
    for c in a_copies:
        c.start()

    def meta_copy(rel):
        return pltpu.make_async_copy(meta_v.at[rel], meta_s.at[rel], local.at[1 + rel])

    def meta_out(rel):
        meta_v[rel] = G[rel, 0:META, :].astype(F32).astype(I32)[0:8]
        meta_copy(rel).start()

    def products(rel, pieces):
        where = [jnp.clip(meta_s[rel, j, 0], 0, C - 1) for j in range(V)]
        wide = jnp.concatenate([G[rel, META + j * B:META + (j + 1) * B, :] for j in range(V)], axis=1)
        for r in pieces:
            tiles = jnp.concatenate([A[r][:, where[j]].reshape(2 * B, B) for j in range(V)], axis=1)
            total = lax.dot_general(tiles, wide, (((1,), (1,)), ((), ())), preferred_element_type=F32)
            partial[rel, r] = total.astype(BF16)

    meta_out(0)
    seen, crossed = [0], []
    for s in range(far - 1):
        for h in range(V):
            for chain in (to_right, to_left):
                chain[s][h].wait_recv()
                if h in chain[s + 1]:
                    chain[s + 1][h].start()
        meta_out(Z - 1 - s)
        meta_out(s + 1)
        if s == far - 4:
            a_copies[0].wait_recv()
            a_on_right.start()
            a_copies[1].wait_recv()
            a_on_left.start()
        if s == far - 3:
            a_copies[2].wait_recv()
            a_copies[3].wait_recv()
        now = [0] if s == 0 else [Z - s, s]
        for rel in now:
            meta_copy(rel).wait()
            products(rel, (0,))
        if s >= far - 3:
            for rel in [rel for rel in seen if rel not in crossed]:
                products(rel, (1, 3))
                crossed.append(rel)
        seen += [Z - 1 - s, s + 1]
    for rel in seen[-2:]:
        meta_copy(rel).wait()
        products(rel, (0,))
    for rel in [rel for rel in seen if rel not in crossed]:
        products(rel, (1, 3))
    a_on_right.wait_recv()
    a_on_left.wait_recv()
    for rel in seen:
        products(rel, (2,))
    for chain in (to_right, to_left):
        for h, c in chain[far - 1].items():
            c.wait_recv()
            if h == 0:
                meta_out(far)
    meta_copy(far).wait()
    products(far, range(X))

    far_y = Y // 2

    def piece_copy(r):
        return copy(part_out.at[0, r], part_in.at[0, r], f_send.at[0], f_recv.at[r], partner)

    def part_copy(n):
        return copy(part_out.at[n], part_in.at[n], p_send.at[0], p_recv.at[n], partner)

    def ring_copy(s, way, r):
        return copy(
            ring_out.at[way, s, r], ring_in.at[way, s, r], r_send.at[0 if s == 0 else 1 + way], r_recv.at[way, s, r],
            at_y(1 if way == 0 else Y - 1),
        )

    def slot_of(n):
        if isinstance(n, int) and n < 2:
            return (y + far_y) % Y if n == 0 else y
        s, way = n // 2, n % 2
        return (y + far_y + (2 * way - 1) * s + Y) % Y

    def source_of(n, whose):
        named = table_s[slot_of(n) * 2 + (core + whose) % 2, 0]
        rel = jnp.clip(named - 1, 0, Z - 1) - z
        return jnp.where(rel < 0, rel + Z, rel), jnp.where(named > 0, 1.0, 0.0).astype(F32)

    def stage(n):
        rel, filled = source_of(n, 1)
        part_out[n] = partial[rel] * filled.astype(BF16)
        part_copy(n).start()

    rel, filled = source_of(0, 1)
    for r in (2, 1, 0, 3):
        part_out[0, r] = partial[rel, r] * filled.astype(BF16)
        piece_copy(r).start()
    rel_0, filled_0 = source_of(0, 0)
    stage(2)
    stage(3)
    for k in range(2):
        for way in range(2):
            r = LATE[way][k]
            piece_copy(r).wait_recv()
            ring_out[way, 0, r] = (partial[rel_0, r].astype(F32) * filled_0 + part_in[0, r].astype(F32)).astype(BF16)
            ring_copy(0, way, r).start()
    for n in (*range(4, Y), 1):
        stage(n)

    def last_copy(way, r):
        if way == 2:
            source, to = own_out.at[r], at_x(r)
        else:
            source, to = ring_out.at[way, far_y - 1, r], at_xy(r, 1 if way == 0 else Y - 1)
        return copy(source, met.at[way, (X - r) % X], m_send.at[way], m_recv.at[way], to)

    def ring_sums(s, way, r, source):
        rel, filled = source
        own = partial[rel, r].astype(F32) * filled
        sums = own + part_in[2 * s + way, r].astype(F32)
        if s > 1 or r in LATE[way]:
            sums = sums + ring_in[way, s - 1, r].astype(F32)
        return sums.astype(BF16)

    def ring_step(s):
        part_copy(2 * s).wait_recv()
        part_copy(2 * s + 1).wait_recv()
        sources = [source_of(2 * s + way, 0) for way in range(2)]
        for way, r in ORDER:
            if r in LATE[way]:
                ring_copy(s - 1, way, r).wait_recv()
            elif s > 1:
                ring_copy(s - 1, way, r).wait_recv()
            ring_out[way, s, r] = ring_sums(s, way, r, sources[way])
            ring_copy(s, way, r).start()

    last = far_y - 1
    for s in range(1, last):
        ring_step(s)
    part_copy(1).wait_recv()
    rel_1, filled_1 = source_of(1, 0)
    for r in (2, 1, 3, 0):
        sums = (partial[rel_1, r].astype(F32) * filled_1 + part_in[1, r].astype(F32)).astype(BF16)
        if r == 0:
            met[2, 0] = sums
        else:
            own_out[r] = sums
            last_copy(2, r).start()
    part_copy(2 * last).wait_recv()
    part_copy(2 * last + 1).wait_recv()
    sources = [source_of(2 * last + way, 0) for way in range(2)]
    for way, r in ORDER:
        ring_copy(last - 1, way, r).wait_recv()
        ring_out[way, last, r] = ring_sums(last, way, r, sources[way])
        last_copy(way, r).start()

    def left(ref, sem):
        copy(ref, ref, sem, f_recv.at[0], partner).wait_send()

    for h in range(V):
        xi_all(h).wait_send()
    for k in range(3):
        left(A0, a_send.at[k])
    for chain, side in ((to_right, 0), (to_left, 1)):
        left(G.at[0:far - 1], z_send.at[side, 0])
        left(G.at[0, 0:sum(PARTS[h][1] for h in chain[far - 1])], z_send.at[side, 1])
    left(part_out.at[0], f_send.at[0])
    left(part_out.at[1:Y], p_send.at[0])
    left(ring_out.at[0, 0], r_send.at[0])
    for way in range(2):
        left(ring_out.at[way, 1:last], r_send.at[1 + way])

    def met_all(way):
        ref = met.at[way] if way < 2 else met.at[2, 1:X]
        return copy(ref, ref, m_send.at[way], m_recv.at[way], partner)

    for way in (2, 0, 1):
        met_all(way).wait_recv()
    slots = out.shape[1]
    for t in range(slots):
        named = table_s[2 * Y + t, 0]
        filled = jnp.where(named > 0, 1.0, 0.0).astype(F32)
        rel = jnp.clip(named - 1, 0, X - 1) - x
        rel = jnp.where(rel < 0, rel + X, rel)
        tiles = (filled * (met[0, rel].astype(F32) + met[1, rel].astype(F32) + met[2, rel].astype(F32))).astype(BF16)
        for i in range(2):
            out[i, t] = tiles[i * B:(i + 1) * B]

    for way in range(3):
        met_all(way).wait_send()


def per_device(Z, Y, amplitudes, amplitude_mask, integrals, integral_mask, owners):
    vmem = pl.BlockSpec(memory_space=pltpu.VMEM)
    smem = pl.BlockSpec(memory_space=pltpu.SMEM)
    hbm = pl.BlockSpec(memory_space=pl.ANY)
    dma = pltpu.SemaphoreType.DMA
    far, far_y = Z // 2, Y // 2
    piece = 2 * B
    return pl.pallas_call(
        functools.partial(kernel, Z, Y),
        out_shape=jax.ShapeDtypeStruct((2, 4, B, B), BF16),
        in_specs=[hbm, smem, hbm, smem, vmem],
        out_specs=vmem,
        scratch_shapes=[
            pltpu.VMEM((2, C, B, B), BF16),
            pltpu.VMEM((1, C, B, B), BF16),
            *[pltpu.VMEM((2, C, B, B), BF16)] * X,
            *[pltpu.VMEM((X, rows, B), BF16) for _, rows in PARTS],
            pltpu.VMEM((Z, UNIT, B), BF16),
            pltpu.VMEM((Z, X, piece, B), BF16),
            pltpu.VMEM((Y, X, piece, B), BF16),
            pltpu.VMEM((Y, X, piece, B), BF16),
            pltpu.VMEM((2, far_y, X, piece, B), BF16),
            pltpu.VMEM((2, far_y - 1, X, piece, B), BF16),
            pltpu.VMEM((X, piece, B), BF16),
            pltpu.VMEM((3, X, piece, B), BF16),
            pltpu.VMEM((TABLE, 128), I32),
            pltpu.SMEM((TABLE, 128), I32),
            pltpu.VMEM((Z, 8, 128), I32),
            pltpu.SMEM((Z, 8, 128), I32),
            dma((V,)), dma((V,)),
            dma((3,)), dma((6,)),
            dma((2, 2)), dma((2, far, V)),
            dma((1,)), dma((X,)),
            dma((1,)), dma((Y,)),
            dma((3,)), dma((2, far_y - 1, X)),
            dma((3,)), dma((3,)),
            dma((3 + Z,)),
        ],
        compiler_params=pltpu.CompilerParams(
            collective_id=0, has_side_effects=True, vmem_limit_bytes=56 * 1024 * 1024),
        cost_estimate=pl.CostEstimate(flops=2 * 128 * 4 * B * B * B, bytes_accessed=1 << 20, transcendentals=0),
    )(amplitudes, amplitude_mask, integrals, integral_mask, owners.reshape(1, -1))


def solution(mesh):
    Z, Y = mesh.shape["row"] // X, mesh.shape["col"] // 2
    return jax.shard_map(
        functools.partial(per_device, Z, Y),
        mesh=mesh,
        in_specs=(
            P("row", "col", None, None),
            P("row", "col"),
            P("row", "col", None, None),
            P("row", "col"),
            P(),
        ),
        out_specs=P("row", "col", None, None),
        check_vma=False,
    )
```

```python
import functools

import jax
import jax.numpy as jnp
from jax import lax
from jax.experimental import pallas as pl
from jax.experimental.pallas import tpu as pltpu
from jax.sharding import PartitionSpec as P


B = 128
X = 4
C = 8
V = 4
META = 16
UNIT = V * B + META
PARTS = [(0, META + B)] + [(META + j * B, B) for j in range(1, V)]
F32 = jnp.float32
BF16 = jnp.bfloat16
I32 = jnp.int32


def orbit_colour(left, right, eye, row, col):
    step = jnp.dot(right.astype(BF16), left.astype(BF16), preferred_element_type=F32)
    reach = jnp.minimum(step + eye, 1.0)
    for _ in range(5):
        half = reach.astype(BF16)
        reach = jnp.minimum(jnp.dot(half, half, preferred_element_type=F32), 1.0)
    label_r = jnp.min(jnp.where(reach > 0.5, row, 999.0), axis=0, keepdims=True)
    label_c = jnp.min(jnp.where(reach > 0.5, col, 999.0), axis=1, keepdims=True)
    other_r = jnp.sum(left * label_c, axis=0, keepdims=True)
    other_c = jnp.sum(left * label_r, axis=1, keepdims=True)
    return jnp.where(label_r > other_r, 1.0, 0.0), jnp.where(label_c > other_c, 1.0, 0.0)


def flip(value):
    return value + 1.0 - 2.0 * (value - 2.0 * jnp.floor(value * 0.5))


def colours_of(owners):
    n = owners.shape[1]
    row_i = lax.broadcasted_iota(I32, (n, n), 0)
    col_i = lax.broadcasted_iota(I32, (n, n), 1)
    row, col = row_i.astype(F32), col_i.astype(F32)
    one = lambda cond: jnp.where(cond, 1.0, 0.0)
    eye = one(row_i == col_i)
    before_r, before_c = one(row_i < col_i), one(col_i < row_i)
    own_r = jnp.broadcast_to(owners, (n, n))
    own_c = jnp.sum(own_r * eye, axis=1, keepdims=True)
    same = one(own_c == own_r)
    over0 = lambda v: jnp.sum(v, axis=0, keepdims=True)
    over1 = lambda v: jnp.sum(v, axis=1, keepdims=True)
    rank_r, rank_c = over0(same * before_r), over1(same * before_c)
    count_r, count_c = over0(same), over1(same)
    even_r, even_c = one(flip(rank_r) > rank_r), one(flip(rank_c) > rank_c)
    lone_r, lone_c = even_r * one(rank_r == count_r - 1.0), even_c * one(rank_c == count_c - 1.0)
    nth_r, nth_c = over0(lone_c * before_r), over1(lone_r * before_c)
    left = one(row_i == (col_i ^ 1))
    right = same * one(rank_c == flip(rank_r)) + lone_c * lone_r * one(nth_c == flip(nth_r))
    first_r, first_c = orbit_colour(left, right, eye, row, col)
    alike = one(first_c == first_r)
    apart = 1.0 - eye
    left = one((row_i // X) == (col_i // X)) * alike * apart
    right = same * alike * apart
    lone_r, lone_c = 1.0 - over0(right), 1.0 - over1(right)
    nth_r, nth_c = over0(lone_c * alike * before_r), over1(lone_r * alike * before_c)
    right = right + lone_c * lone_r * alike * one(nth_c == flip(nth_r))
    second_r, _ = orbit_colour(left, right, eye, row, col)
    return 2.0 * first_r + second_r, rank_r


TABLE = 40


def table_of(owners, me_x, me_z, me_col, cols):
    own = owners.astype(F32)
    colour, rank = colours_of(own)
    n = owners.shape[1]

    def part(rows, make):
        at = lax.broadcasted_iota(I32, (rows, n), 0).astype(F32)
        edge = lax.broadcasted_iota(I32, (rows, n), 1)
        return jnp.sum(make(at, (edge // X).astype(F32), (edge % X).astype(F32)), axis=1, keepdims=True)

    x, z, d = me_x.astype(F32), me_z.astype(F32), me_col.astype(F32)
    slots = part(cols, lambda at, ez, ex: jnp.where((own == at) & (colour == x), ez + 1.0, 0.0))
    mine = part(8, lambda at, ez, ex: jnp.where((rank == at) & (own == d), colour + 1.0, 0.0))
    unit = part(8, lambda at, ez, ex: jnp.where((colour == x) & (ez == z), ex, 0.0))
    spare = jnp.zeros((TABLE - cols - 16, 1), F32)
    rows = jnp.concatenate([slots, mine, unit, spare], axis=0)
    return jnp.broadcast_to(rows, (TABLE, 128)).astype(I32)


LATE = ((2, 0), (1, 3))
ORDER = [(way, LATE[1 - way][k] if early else LATE[way][k])
         for early in (True, False) for k in range(2) for way in range(2)]


def kernel(
    Z, Y, amp_hbm, amp_mask, int_hbm, int_mask, owners, out,
    amp, integral, A0, A1, A2, A3, XI0, XI1, XI2, XI3, G, partial, part_out, part_in, ring_out, ring_in, own_out, met, table_v, table_s, meta_v, meta_s,
    xi_send, xi_recv, a_send, a_recv, z_send, z_recv, f_send, f_recv, p_send, p_recv, r_send, r_recv, m_send, m_recv, local,
):
    row, col = lax.axis_index("row"), lax.axis_index("col")
    x, z, y, core = row % X, row // X, col // 2, col % 2

    def at_x(shift):
        return (z * X + (x + shift) % X, col)

    def at_z(shift):
        return (((z + shift) % Z) * X + x, col)

    def at_y(shift):
        return (row, ((y + shift) % Y) * 2 + core)

    def at_xy(right, up):
        return (z * X + (x + right) % X, ((y + up) % Y) * 2 + core)

    partner = (row, y * 2 + (1 - core))

    barrier = pltpu.get_barrier_semaphore()
    peers = [at_x(1), at_x(2), at_x(3), at_z(1), at_z(Z - 1), at_y(1), at_y(Y - 1), partner]
    peers += [at_xy(r, up) for r in range(1, X) for up in (1, Y - 1)]
    for peer in peers:
        pl.semaphore_signal(barrier, inc=1, device_id=peer, device_id_type=pl.DeviceIdType.MESH)

    int_in = pltpu.make_async_copy(int_hbm, integral, local.at[Z + 1])
    amp_in = pltpu.make_async_copy(amp_hbm, amp, local.at[Z + 2])
    int_in.start()
    amp_in.start()

    def copy(src, dst, send, recv, to):
        return pltpu.make_async_remote_copy(
            src_ref=src, dst_ref=dst, send_sem=send, recv_sem=recv, device_id=to,
            device_id_type=pl.DeviceIdType.MESH,
        )

    int_in.wait()
    kept = [int_mask[0, c] for c in range(C)]
    before, places = jnp.int32(0), [jnp.int32(0)] * V
    for c in range(C):
        for j in range(V):
            places[j] = jnp.where((kept[c] != 0) & (before == j), c, places[j])
        before = before + kept[c]
    XI = (XI0, XI1, XI2, XI3)
    at = lax.broadcasted_iota(I32, (META, B), 0)
    meta = jnp.zeros((META, B), I32)
    for j in range(V):
        meta = jnp.where(at == j, places[j], meta)
    XI0[0, 0:META] = meta.astype(F32).astype(BF16)
    for j in range(V):
        scale = jnp.where(before > j, 1.0, 0.0).astype(BF16)
        first = META if j == 0 else 0
        XI[j][0, first:first + B] = integral[0, places[j]] * scale

    pl.semaphore_wait(barrier, len(peers))

    xi_copies = [
        [copy(XI[h].at[0], XI[h].at[X - r], xi_send.at[h], xi_recv.at[h], at_x(r)) for r in (1, 3, 2)]
        for h in range(V)
    ]

    def xi_all(h):
        return copy(XI[h].at[1:X], XI[h].at[1:X], xi_send.at[h], xi_recv.at[h], at_x(1))

    for h in range(V):
        for c in xi_copies[h]:
            c.start()

    amp_in.wait()
    for i in range(2):
        for c in range(C):
            A0[i, c] = amp[i, c] * amp_mask[i, c].astype(F32).astype(BF16)

    A = (A0, A1, A2, A3)
    a_copies = [
        copy(A0.at[0], A3.at[0], a_send.at[0], a_recv.at[0], at_x(1)),
        copy(A0.at[1], A1.at[1], a_send.at[0], a_recv.at[1], at_x(3)),
        copy(A0.at[1], A3.at[1], a_send.at[1], a_recv.at[2], at_x(1)),
        copy(A0.at[0], A1.at[0], a_send.at[1], a_recv.at[3], at_x(3)),
    ]
    a_on_right = copy(A3.at[0], A2.at[0], a_send.at[2], a_recv.at[4], at_x(1))
    a_on_left = copy(A1.at[1], A2.at[1], a_send.at[2], a_recv.at[5], at_x(3))

    table_v[...] = table_of(owners[...], x, z, col, 2 * Y)
    table_copy = pltpu.make_async_copy(table_v, table_s, local.at[0])
    table_copy.start()

    far = Z // 2
    RIGHT, LEFT = range(0, V // 2), range(V // 2, V)

    def rows_of(h):
        return pl.ds(*PARTS[h])

    to_right = [
        {h: copy(G.at[(Z - s) % Z, rows_of(h)], G.at[Z - 1 - s, rows_of(h)], z_send.at[0, s // (far - 1)], z_recv.at[0, s, h], at_z(1))
         for h in (range(V) if s < far - 1 else RIGHT)}
        for s in range(far)
    ]
    to_left = [
        {h: copy(G.at[s, rows_of(h)], G.at[s + 1, rows_of(h)], z_send.at[1, s // (far - 1)], z_recv.at[1, s, h], at_z(Z - 1))
         for h in (range(V) if s < far - 1 else LEFT)}
        for s in range(far)
    ]

    table_copy.wait()
    from_rel = (jnp.clip(table_s[2 * Y + 8, 0], 0, X - 1) - x + X) % X
    for h in range(V):
        xi_all(h).wait_recv()
        G[0, rows_of(h)] = XI[h][from_rel]
        to_right[0][h].start()
        to_left[0][h].start()
    for c in a_copies:
        c.start()

    def meta_copy(rel):
        return pltpu.make_async_copy(meta_v.at[rel], meta_s.at[rel], local.at[1 + rel])

    def meta_out(rel):
        meta_v[rel] = G[rel, 0:META, :].astype(F32).astype(I32)[0:8]
        meta_copy(rel).start()

    def products(rel, pieces):
        where = [jnp.clip(meta_s[rel, j, 0], 0, C - 1) for j in range(V)]
        wide = jnp.concatenate([G[rel, META + j * B:META + (j + 1) * B, :] for j in range(V)], axis=1)
        for r in pieces:
            tiles = jnp.concatenate([A[r][:, where[j]].reshape(2 * B, B) for j in range(V)], axis=1)
            total = lax.dot_general(tiles, wide, (((1,), (1,)), ((), ())), preferred_element_type=F32)
            partial[rel, r] = total.astype(BF16)

    meta_out(0)
    seen, crossed = [0], []
    for s in range(far - 1):
        for h in range(V):
            for chain in (to_right, to_left):
                chain[s][h].wait_recv()
                if h in chain[s + 1]:
                    chain[s + 1][h].start()
        meta_out(Z - 1 - s)
        meta_out(s + 1)
        if s == far - 4:
            a_copies[0].wait_recv()
            a_on_right.start()
            a_copies[1].wait_recv()
            a_on_left.start()
        if s == far - 3:
            a_copies[2].wait_recv()
            a_copies[3].wait_recv()
        now = [0] if s == 0 else [Z - s, s]
        for rel in now:
            meta_copy(rel).wait()
            products(rel, (0,))
        if s >= far - 3:
            for rel in [rel for rel in seen if rel not in crossed]:
                products(rel, (1, 3))
                crossed.append(rel)
        seen += [Z - 1 - s, s + 1]
    for rel in seen[-2:]:
        meta_copy(rel).wait()
        products(rel, (0,))
    for rel in [rel for rel in seen if rel not in crossed]:
        products(rel, (1, 3))
    a_on_right.wait_recv()
    a_on_left.wait_recv()
    for rel in seen:
        products(rel, (2,))
    for chain in (to_right, to_left):
        for h, c in chain[far - 1].items():
            c.wait_recv()
            if h == 0:
                meta_out(far)
    meta_copy(far).wait()
    products(far, range(X))

    far_y = Y // 2

    def piece_copy(r):
        return copy(part_out.at[0, r], part_in.at[0, r], f_send.at[0], f_recv.at[r], partner)

    def part_copy(n):
        return copy(part_out.at[n], part_in.at[n], p_send.at[0], p_recv.at[n], partner)

    def ring_copy(s, way, r):
        return copy(
            ring_out.at[way, s, r], ring_in.at[way, s, r], r_send.at[0 if s == 0 else 1 + way], r_recv.at[way, s, r],
            at_y(1 if way == 0 else Y - 1),
        )

    def slot_of(n):
        if isinstance(n, int) and n < 2:
            return (y + far_y) % Y if n == 0 else y
        s, way = n // 2, n % 2
        return (y + far_y + (2 * way - 1) * s + Y) % Y

    def source_of(n, whose):
        named = table_s[slot_of(n) * 2 + (core + whose) % 2, 0]
        rel = jnp.clip(named - 1, 0, Z - 1) - z
        return jnp.where(rel < 0, rel + Z, rel), jnp.where(named > 0, 1.0, 0.0).astype(F32)

    def stage(n):
        rel, filled = source_of(n, 1)
        part_out[n] = partial[rel] * filled.astype(BF16)
        part_copy(n).start()

    rel, filled = source_of(0, 1)
    for r in (2, 1, 0, 3):
        part_out[0, r] = partial[rel, r] * filled.astype(BF16)
        piece_copy(r).start()
    rel_0, filled_0 = source_of(0, 0)
    for k in range(2):
        for way in range(2):
            r = LATE[way][k]
            piece_copy(r).wait_recv()
            ring_out[way, 0, r] = (partial[rel_0, r].astype(F32) * filled_0 + part_in[0, r].astype(F32)).astype(BF16)
            ring_copy(0, way, r).start()
    for n in (2, 3, *range(4, Y), 1):
        stage(n)

    def last_copy(way, r):
        if way == 2:
            source, to = own_out.at[r], at_x(r)
        else:
            source, to = ring_out.at[way, far_y - 1, r], at_xy(r, 1 if way == 0 else Y - 1)
        return copy(source, met.at[way, (X - r) % X], m_send.at[way], m_recv.at[way], to)

    def ring_sums(s, way, r, source):
        rel, filled = source
        own = partial[rel, r].astype(F32) * filled
        sums = own + part_in[2 * s + way, r].astype(F32)
        if s > 1 or r in LATE[way]:
            sums = sums + ring_in[way, s - 1, r].astype(F32)
        return sums.astype(BF16)

    def ring_step(s):
        part_copy(2 * s).wait_recv()
        part_copy(2 * s + 1).wait_recv()
        sources = [source_of(2 * s + way, 0) for way in range(2)]
        for way, r in ORDER:
            if r in LATE[way]:
                ring_copy(s - 1, way, r).wait_recv()
            elif s > 1:
                ring_copy(s - 1, way, r).wait_recv()
            ring_out[way, s, r] = ring_sums(s, way, r, sources[way])
            ring_copy(s, way, r).start()

    last = far_y - 1
    for s in range(1, last):
        ring_step(s)
    part_copy(1).wait_recv()
    rel_1, filled_1 = source_of(1, 0)
    for r in (2, 1, 3, 0):
        sums = (partial[rel_1, r].astype(F32) * filled_1 + part_in[1, r].astype(F32)).astype(BF16)
        if r == 0:
            met[2, 0] = sums
        else:
            own_out[r] = sums
            last_copy(2, r).start()
    part_copy(2 * last).wait_recv()
    part_copy(2 * last + 1).wait_recv()
    sources = [source_of(2 * last + way, 0) for way in range(2)]
    for way, r in ORDER:
        ring_copy(last - 1, way, r).wait_recv()
        ring_out[way, last, r] = ring_sums(last, way, r, sources[way])
        last_copy(way, r).start()

    def left(ref, sem):
        copy(ref, ref, sem, f_recv.at[0], partner).wait_send()

    for h in range(V):
        xi_all(h).wait_send()
    for k in range(3):
        left(A0, a_send.at[k])
    for chain, side in ((to_right, 0), (to_left, 1)):
        left(G.at[0:far - 1], z_send.at[side, 0])
        left(G.at[0, 0:sum(PARTS[h][1] for h in chain[far - 1])], z_send.at[side, 1])
    left(part_out.at[0], f_send.at[0])
    left(part_out.at[1:Y], p_send.at[0])
    left(ring_out.at[0, 0], r_send.at[0])
    for way in range(2):
        left(ring_out.at[way, 1:last], r_send.at[1 + way])

    def met_all(way):
        ref = met.at[way] if way < 2 else met.at[2, 1:X]
        return copy(ref, ref, m_send.at[way], m_recv.at[way], partner)

    for way in (2, 0, 1):
        met_all(way).wait_recv()
    slots = out.shape[1]
    for t in range(slots):
        named = table_s[2 * Y + t, 0]
        filled = jnp.where(named > 0, 1.0, 0.0).astype(F32)
        rel = jnp.clip(named - 1, 0, X - 1) - x
        rel = jnp.where(rel < 0, rel + X, rel)
        tiles = (filled * (met[0, rel].astype(F32) + met[1, rel].astype(F32) + met[2, rel].astype(F32))).astype(BF16)
        for i in range(2):
            out[i, t] = tiles[i * B:(i + 1) * B]

    for way in range(3):
        met_all(way).wait_send()


def per_device(Z, Y, amplitudes, amplitude_mask, integrals, integral_mask, owners):
    vmem = pl.BlockSpec(memory_space=pltpu.VMEM)
    smem = pl.BlockSpec(memory_space=pltpu.SMEM)
    hbm = pl.BlockSpec(memory_space=pl.ANY)
    dma = pltpu.SemaphoreType.DMA
    far, far_y = Z // 2, Y // 2
    piece = 2 * B
    return pl.pallas_call(
        functools.partial(kernel, Z, Y),
        out_shape=jax.ShapeDtypeStruct((2, 4, B, B), BF16),
        in_specs=[hbm, smem, hbm, smem, vmem],
        out_specs=vmem,
        scratch_shapes=[
            pltpu.VMEM((2, C, B, B), BF16),
            pltpu.VMEM((1, C, B, B), BF16),
            *[pltpu.VMEM((2, C, B, B), BF16)] * X,
            *[pltpu.VMEM((X, rows, B), BF16) for _, rows in PARTS],
            pltpu.VMEM((Z, UNIT, B), BF16),
            pltpu.VMEM((Z, X, piece, B), BF16),
            pltpu.VMEM((Y, X, piece, B), BF16),
            pltpu.VMEM((Y, X, piece, B), BF16),
            pltpu.VMEM((2, far_y, X, piece, B), BF16),
            pltpu.VMEM((2, far_y - 1, X, piece, B), BF16),
            pltpu.VMEM((X, piece, B), BF16),
            pltpu.VMEM((3, X, piece, B), BF16),
            pltpu.VMEM((TABLE, 128), I32),
            pltpu.SMEM((TABLE, 128), I32),
            pltpu.VMEM((Z, 8, 128), I32),
            pltpu.SMEM((Z, 8, 128), I32),
            dma((V,)), dma((V,)),
            dma((3,)), dma((6,)),
            dma((2, 2)), dma((2, far, V)),
            dma((1,)), dma((X,)),
            dma((1,)), dma((Y,)),
            dma((3,)), dma((2, far_y - 1, X)),
            dma((3,)), dma((3,)),
            dma((3 + Z,)),
        ],
        compiler_params=pltpu.CompilerParams(
            collective_id=0, has_side_effects=True, vmem_limit_bytes=56 * 1024 * 1024),
        cost_estimate=pl.CostEstimate(flops=2 * 128 * 4 * B * B * B, bytes_accessed=1 << 20, transcendentals=0),
    )(amplitudes, amplitude_mask, integrals, integral_mask, owners.reshape(1, -1))


def solution(mesh):
    Z, Y = mesh.shape["row"] // X, mesh.shape["col"] // 2
    return jax.shard_map(
        functools.partial(per_device, Z, Y),
        mesh=mesh,
        in_specs=(
            P("row", "col", None, None),
            P("row", "col"),
            P("row", "col", None, None),
            P("row", "col"),
            P(),
        ),
        out_specs=P("row", "col", None, None),
        check_vma=False,
    )
```

```python
import functools

import jax
import jax.numpy as jnp
from jax import lax
from jax.experimental import pallas as pl
from jax.experimental.pallas import tpu as pltpu
from jax.sharding import PartitionSpec as P


B = 128
X = 4
C = 8
V = 4
META = 16
UNIT = V * B + META
PARTS = [(0, META + B)] + [(META + j * B, B) for j in range(1, V)]
F32 = jnp.float32
BF16 = jnp.bfloat16
I32 = jnp.int32


def orbit_colour(left, right, eye, row, col):
    step = jnp.dot(right.astype(BF16), left.astype(BF16), preferred_element_type=F32)
    reach = jnp.minimum(step + eye, 1.0)
    for _ in range(5):
        half = reach.astype(BF16)
        reach = jnp.minimum(jnp.dot(half, half, preferred_element_type=F32), 1.0)
    label_r = jnp.min(jnp.where(reach > 0.5, row, 999.0), axis=0, keepdims=True)
    label_c = jnp.min(jnp.where(reach > 0.5, col, 999.0), axis=1, keepdims=True)
    other_r = jnp.sum(left * label_c, axis=0, keepdims=True)
    other_c = jnp.sum(left * label_r, axis=1, keepdims=True)
    return jnp.where(label_r > other_r, 1.0, 0.0), jnp.where(label_c > other_c, 1.0, 0.0)


def flip(value):
    return value + 1.0 - 2.0 * (value - 2.0 * jnp.floor(value * 0.5))


def colours_of(owners):
    n = owners.shape[1]
    row_i = lax.broadcasted_iota(I32, (n, n), 0)
    col_i = lax.broadcasted_iota(I32, (n, n), 1)
    row, col = row_i.astype(F32), col_i.astype(F32)
    one = lambda cond: jnp.where(cond, 1.0, 0.0)
    eye = one(row_i == col_i)
    before_r, before_c = one(row_i < col_i), one(col_i < row_i)
    own_r = jnp.broadcast_to(owners, (n, n))
    own_c = jnp.sum(own_r * eye, axis=1, keepdims=True)
    same = one(own_c == own_r)
    over0 = lambda v: jnp.sum(v, axis=0, keepdims=True)
    over1 = lambda v: jnp.sum(v, axis=1, keepdims=True)
    rank_r, rank_c = over0(same * before_r), over1(same * before_c)
    count_r, count_c = over0(same), over1(same)
    even_r, even_c = one(flip(rank_r) > rank_r), one(flip(rank_c) > rank_c)
    lone_r, lone_c = even_r * one(rank_r == count_r - 1.0), even_c * one(rank_c == count_c - 1.0)
    nth_r, nth_c = over0(lone_c * before_r), over1(lone_r * before_c)
    left = one(row_i == (col_i ^ 1))
    right = same * one(rank_c == flip(rank_r)) + lone_c * lone_r * one(nth_c == flip(nth_r))
    first_r, first_c = orbit_colour(left, right, eye, row, col)
    alike = one(first_c == first_r)
    apart = 1.0 - eye
    left = one((row_i // X) == (col_i // X)) * alike * apart
    right = same * alike * apart
    lone_r, lone_c = 1.0 - over0(right), 1.0 - over1(right)
    nth_r, nth_c = over0(lone_c * alike * before_r), over1(lone_r * alike * before_c)
    right = right + lone_c * lone_r * alike * one(nth_c == flip(nth_r))
    second_r, _ = orbit_colour(left, right, eye, row, col)
    return 2.0 * first_r + second_r, rank_r


TABLE = 40


def table_of(owners, me_x, me_z, me_col, cols):
    own = owners.astype(F32)
    colour, rank = colours_of(own)
    n = owners.shape[1]

    def part(rows, make):
        at = lax.broadcasted_iota(I32, (rows, n), 0).astype(F32)
        edge = lax.broadcasted_iota(I32, (rows, n), 1)
        return jnp.sum(make(at, (edge // X).astype(F32), (edge % X).astype(F32)), axis=1, keepdims=True)

    x, z, d = me_x.astype(F32), me_z.astype(F32), me_col.astype(F32)
    slots = part(cols, lambda at, ez, ex: jnp.where((own == at) & (colour == x), ez + 1.0, 0.0))
    mine = part(8, lambda at, ez, ex: jnp.where((rank == at) & (own == d), colour + 1.0, 0.0))
    unit = part(8, lambda at, ez, ex: jnp.where((colour == x) & (ez == z), ex, 0.0))
    spare = jnp.zeros((TABLE - cols - 16, 1), F32)
    rows = jnp.concatenate([slots, mine, unit, spare], axis=0)
    return jnp.broadcast_to(rows, (TABLE, 128)).astype(I32)


LATE = ((2, 0), (1, 3))
SPOT = {2: 0, 0: 1, 1: 2, 3: 3}


def kernel(
    Z, Y, amp_hbm, amp_mask, int_hbm, int_mask, owners, out,
    amp, integral, A0, A1, A2, A3, XI0, XI1, XI2, XI3, G, partial, part_out, part_in, ring_out, ring_in, own_out, met, table_v, table_s, meta_v, meta_s,
    xi_send, xi_recv, a_send, a_recv, z_send, z_recv, f_send, f_recv, p_send, p_recv, r_send, r_recv, m_send, m_recv, local,
):
    row, col = lax.axis_index("row"), lax.axis_index("col")
    x, z, y, core = row % X, row // X, col // 2, col % 2

    def at_x(shift):
        return (z * X + (x + shift) % X, col)

    def at_z(shift):
        return (((z + shift) % Z) * X + x, col)

    def at_y(shift):
        return (row, ((y + shift) % Y) * 2 + core)

    def at_xy(right, up):
        return (z * X + (x + right) % X, ((y + up) % Y) * 2 + core)

    partner = (row, y * 2 + (1 - core))

    barrier = pltpu.get_barrier_semaphore()
    peers = [at_x(1), at_x(2), at_x(3), at_z(1), at_z(Z - 1), at_y(1), at_y(Y - 1), partner]
    peers += [at_xy(r, up) for r in range(1, X) for up in (1, Y - 1)]
    for peer in peers:
        pl.semaphore_signal(barrier, inc=1, device_id=peer, device_id_type=pl.DeviceIdType.MESH)

    int_in = pltpu.make_async_copy(int_hbm, integral, local.at[Z + 1])
    amp_in = pltpu.make_async_copy(amp_hbm, amp, local.at[Z + 2])
    int_in.start()
    amp_in.start()

    def copy(src, dst, send, recv, to):
        return pltpu.make_async_remote_copy(
            src_ref=src, dst_ref=dst, send_sem=send, recv_sem=recv, device_id=to,
            device_id_type=pl.DeviceIdType.MESH,
        )

    int_in.wait()
    kept = [int_mask[0, c] for c in range(C)]
    before, places = jnp.int32(0), [jnp.int32(0)] * V
    for c in range(C):
        for j in range(V):
            places[j] = jnp.where((kept[c] != 0) & (before == j), c, places[j])
        before = before + kept[c]
    XI = (XI0, XI1, XI2, XI3)
    at = lax.broadcasted_iota(I32, (META, B), 0)
    meta = jnp.zeros((META, B), I32)
    for j in range(V):
        meta = jnp.where(at == j, places[j], meta)
    XI0[0, 0:META] = meta.astype(F32).astype(BF16)
    for j in range(V):
        scale = jnp.where(before > j, 1.0, 0.0).astype(BF16)
        first = META if j == 0 else 0
        XI[j][0, first:first + B] = integral[0, places[j]] * scale

    pl.semaphore_wait(barrier, len(peers))

    xi_copies = [
        [copy(XI[h].at[0], XI[h].at[X - r], xi_send.at[h], xi_recv.at[h], at_x(r)) for r in (1, 3, 2)]
        for h in range(V)
    ]

    def xi_all(h):
        return copy(XI[h].at[1:X], XI[h].at[1:X], xi_send.at[h], xi_recv.at[h], at_x(1))

    for h in range(V):
        for c in xi_copies[h]:
            c.start()

    amp_in.wait()
    for i in range(2):
        for c in range(C):
            A0[i, c] = amp[i, c] * amp_mask[i, c].astype(F32).astype(BF16)

    A = (A0, A1, A2, A3)
    a_copies = [
        copy(A0.at[0], A3.at[0], a_send.at[0], a_recv.at[0], at_x(1)),
        copy(A0.at[1], A1.at[1], a_send.at[0], a_recv.at[1], at_x(3)),
        copy(A0.at[1], A3.at[1], a_send.at[1], a_recv.at[2], at_x(1)),
        copy(A0.at[0], A1.at[0], a_send.at[1], a_recv.at[3], at_x(3)),
    ]
    a_on_right = copy(A3.at[0], A2.at[0], a_send.at[2], a_recv.at[4], at_x(1))
    a_on_left = copy(A1.at[1], A2.at[1], a_send.at[2], a_recv.at[5], at_x(3))

    table_v[...] = table_of(owners[...], x, z, col, 2 * Y)
    table_copy = pltpu.make_async_copy(table_v, table_s, local.at[0])
    table_copy.start()

    far = Z // 2
    RIGHT, LEFT = range(0, V // 2), range(V // 2, V)

    def rows_of(h):
        return pl.ds(*PARTS[h])

    to_right = [
        {h: copy(G.at[(Z - s) % Z, rows_of(h)], G.at[Z - 1 - s, rows_of(h)], z_send.at[0, s // (far - 1)], z_recv.at[0, s, h], at_z(1))
         for h in (range(V) if s < far - 1 else RIGHT)}
        for s in range(far)
    ]
    to_left = [
        {h: copy(G.at[s, rows_of(h)], G.at[s + 1, rows_of(h)], z_send.at[1, s // (far - 1)], z_recv.at[1, s, h], at_z(Z - 1))
         for h in (range(V) if s < far - 1 else LEFT)}
        for s in range(far)
    ]

    table_copy.wait()
    from_rel = (jnp.clip(table_s[2 * Y + 8, 0], 0, X - 1) - x + X) % X
    for h in range(V):
        xi_all(h).wait_recv()
        G[0, rows_of(h)] = XI[h][from_rel]
        to_right[0][h].start()
        to_left[0][h].start()
    for c in a_copies:
        c.start()

    def meta_copy(rel):
        return pltpu.make_async_copy(meta_v.at[rel], meta_s.at[rel], local.at[1 + rel])

    def meta_out(rel):
        meta_v[rel] = G[rel, 0:META, :].astype(F32).astype(I32)[0:8]
        meta_copy(rel).start()

    def products(rel, pieces):
        where = [jnp.clip(meta_s[rel, j, 0], 0, C - 1) for j in range(V)]
        wide = jnp.concatenate([G[rel, META + j * B:META + (j + 1) * B, :] for j in range(V)], axis=1)
        for r in pieces:
            tiles = jnp.concatenate([A[r][:, where[j]].reshape(2 * B, B) for j in range(V)], axis=1)
            total = lax.dot_general(tiles, wide, (((1,), (1,)), ((), ())), preferred_element_type=F32)
            partial[rel, r] = total.astype(BF16)

    meta_out(0)
    seen, crossed = [0], []
    for s in range(far - 1):
        for h in range(V):
            for chain in (to_right, to_left):
                chain[s][h].wait_recv()
                if h in chain[s + 1]:
                    chain[s + 1][h].start()
        meta_out(Z - 1 - s)
        meta_out(s + 1)
        if s == far - 4:
            a_copies[0].wait_recv()
            a_on_right.start()
            a_copies[1].wait_recv()
            a_on_left.start()
        if s == far - 3:
            a_copies[2].wait_recv()
            a_copies[3].wait_recv()
        now = [0] if s == 0 else [Z - s, s]
        for rel in now:
            meta_copy(rel).wait()
            products(rel, (0,))
        if s >= far - 3:
            for rel in [rel for rel in seen if rel not in crossed]:
                products(rel, (1, 3))
                crossed.append(rel)
        seen += [Z - 1 - s, s + 1]
    for rel in seen[-2:]:
        meta_copy(rel).wait()
        products(rel, (0,))
    for rel in [rel for rel in seen if rel not in crossed]:
        products(rel, (1, 3))
    a_on_right.wait_recv()
    a_on_left.wait_recv()
    for rel in seen:
        products(rel, (2,))
    for chain in (to_right, to_left):
        for h, c in chain[far - 1].items():
            c.wait_recv()
            if h == 0:
                meta_out(far)
    meta_copy(far).wait()
    products(far, range(X))

    far_y = Y // 2

    def piece_copy(r):
        return copy(part_out.at[0, r], part_in.at[0, r], f_send.at[0], f_recv.at[r], partner)

    def part_copy(n):
        return copy(part_out.at[n], part_in.at[n], p_send.at[0], p_recv.at[n], partner)

    def ring_copy(s, way, group):
        pieces = pl.ds(2 * group, 2)
        return copy(
            ring_out.at[way, s, pieces], ring_in.at[way, s, pieces], r_send.at[0 if s == 0 else 1 + way],
            r_recv.at[way, s, group], at_y(1 if way == 0 else Y - 1))

    def slot_of(n):
        if isinstance(n, int) and n < 2:
            return (y + far_y) % Y if n == 0 else y
        s, way = n // 2, n % 2
        return (y + far_y + (2 * way - 1) * s + Y) % Y

    def source_of(n, whose):
        named = table_s[slot_of(n) * 2 + (core + whose) % 2, 0]
        rel = jnp.clip(named - 1, 0, Z - 1) - z
        return jnp.where(rel < 0, rel + Z, rel), jnp.where(named > 0, 1.0, 0.0).astype(F32)

    def stage(n):
        rel, filled = source_of(n, 1)
        part_out[n] = partial[rel] * filled.astype(BF16)
        part_copy(n).start()

    rel, filled = source_of(0, 1)
    for r in (2, 1, 0, 3):
        part_out[0, r] = partial[rel, r] * filled.astype(BF16)
        piece_copy(r).start()
    rel_0, filled_0 = source_of(0, 0)
    for way in range(2):
        for r in LATE[way]:
            piece_copy(r).wait_recv()
            ring_out[way, 0, SPOT[r]] = (
                partial[rel_0, r].astype(F32) * filled_0 + part_in[0, r].astype(F32)).astype(BF16)
        ring_copy(0, way, way).start()
    for n in (2, 3, *range(4, Y), 1):
        stage(n)

    def last_copy(way, r):
        if way == 2:
            source, to = own_out.at[r], at_x(r)
        else:
            source, to = ring_out.at[way, far_y - 1, SPOT[r]], at_xy(r, 1 if way == 0 else Y - 1)
        return copy(source, met.at[way, (X - r) % X], m_send.at[way], m_recv.at[way], to)

    def ring_sums(s, way, r, source):
        rel, filled = source
        own = partial[rel, r].astype(F32) * filled
        sums = own + part_in[2 * s + way, r].astype(F32)
        if s > 1 or r in LATE[way]:
            sums = sums + ring_in[way, s - 1, SPOT[r]].astype(F32)
        return sums.astype(BF16)

    def ring_step(s):
        part_copy(2 * s).wait_recv()
        part_copy(2 * s + 1).wait_recv()
        sources = [source_of(2 * s + way, 0) for way in range(2)]
        for late in range(2):
            for way in range(2):
                group = way if late else 1 - way
                if late or s > 1:
                    ring_copy(s - 1, way, group).wait_recv()
                for r in LATE[group]:
                    ring_out[way, s, SPOT[r]] = ring_sums(s, way, r, sources[way])
                ring_copy(s, way, group).start()

    last = far_y - 1
    for s in range(1, last):
        ring_step(s)
    part_copy(1).wait_recv()
    rel_1, filled_1 = source_of(1, 0)
    for r in (2, 1, 3, 0):
        sums = (partial[rel_1, r].astype(F32) * filled_1 + part_in[1, r].astype(F32)).astype(BF16)
        if r == 0:
            met[2, 0] = sums
        else:
            own_out[r] = sums
            last_copy(2, r).start()
    part_copy(2 * last).wait_recv()
    part_copy(2 * last + 1).wait_recv()
    sources = [source_of(2 * last + way, 0) for way in range(2)]
    for late in range(2):
        for way in range(2):
            group = way if late else 1 - way
            ring_copy(last - 1, way, group).wait_recv()
            for r in LATE[group]:
                ring_out[way, last, SPOT[r]] = ring_sums(last, way, r, sources[way])
                last_copy(way, r).start()

    def left(ref, sem):
        copy(ref, ref, sem, f_recv.at[0], partner).wait_send()

    for h in range(V):
        xi_all(h).wait_send()
    for k in range(3):
        left(A0, a_send.at[k])
    for chain, side in ((to_right, 0), (to_left, 1)):
        left(G.at[0:far - 1], z_send.at[side, 0])
        left(G.at[0, 0:sum(PARTS[h][1] for h in chain[far - 1])], z_send.at[side, 1])
    left(part_out.at[0], f_send.at[0])
    left(part_out.at[1:Y], p_send.at[0])
    left(ring_out.at[0, 0], r_send.at[0])
    for way in range(2):
        left(ring_out.at[way, 1:last], r_send.at[1 + way])

    def met_all(way):
        ref = met.at[way] if way < 2 else met.at[2, 1:X]
        return copy(ref, ref, m_send.at[way], m_recv.at[way], partner)

    for way in (2, 0, 1):
        met_all(way).wait_recv()
    slots = out.shape[1]
    for t in range(slots):
        named = table_s[2 * Y + t, 0]
        filled = jnp.where(named > 0, 1.0, 0.0).astype(F32)
        rel = jnp.clip(named - 1, 0, X - 1) - x
        rel = jnp.where(rel < 0, rel + X, rel)
        tiles = (filled * (met[0, rel].astype(F32) + met[1, rel].astype(F32) + met[2, rel].astype(F32))).astype(BF16)
        for i in range(2):
            out[i, t] = tiles[i * B:(i + 1) * B]

    for way in range(3):
        met_all(way).wait_send()


def per_device(Z, Y, amplitudes, amplitude_mask, integrals, integral_mask, owners):
    vmem = pl.BlockSpec(memory_space=pltpu.VMEM)
    smem = pl.BlockSpec(memory_space=pltpu.SMEM)
    hbm = pl.BlockSpec(memory_space=pl.ANY)
    dma = pltpu.SemaphoreType.DMA
    far, far_y = Z // 2, Y // 2
    piece = 2 * B
    return pl.pallas_call(
        functools.partial(kernel, Z, Y),
        out_shape=jax.ShapeDtypeStruct((2, 4, B, B), BF16),
        in_specs=[hbm, smem, hbm, smem, vmem],
        out_specs=vmem,
        scratch_shapes=[
            pltpu.VMEM((2, C, B, B), BF16),
            pltpu.VMEM((1, C, B, B), BF16),
            *[pltpu.VMEM((2, C, B, B), BF16)] * X,
            *[pltpu.VMEM((X, rows, B), BF16) for _, rows in PARTS],
            pltpu.VMEM((Z, UNIT, B), BF16),
            pltpu.VMEM((Z, X, piece, B), BF16),
            pltpu.VMEM((Y, X, piece, B), BF16),
            pltpu.VMEM((Y, X, piece, B), BF16),
            pltpu.VMEM((2, far_y, X, piece, B), BF16),
            pltpu.VMEM((2, far_y - 1, X, piece, B), BF16),
            pltpu.VMEM((X, piece, B), BF16),
            pltpu.VMEM((3, X, piece, B), BF16),
            pltpu.VMEM((TABLE, 128), I32),
            pltpu.SMEM((TABLE, 128), I32),
            pltpu.VMEM((Z, 8, 128), I32),
            pltpu.SMEM((Z, 8, 128), I32),
            dma((V,)), dma((V,)),
            dma((3,)), dma((6,)),
            dma((2, 2)), dma((2, far, V)),
            dma((1,)), dma((X,)),
            dma((1,)), dma((Y,)),
            dma((3,)), dma((2, far_y - 1, 2)),
            dma((3,)), dma((3,)),
            dma((3 + Z,)),
        ],
        compiler_params=pltpu.CompilerParams(
            collective_id=0, has_side_effects=True, vmem_limit_bytes=56 * 1024 * 1024),
        cost_estimate=pl.CostEstimate(flops=2 * 128 * 4 * B * B * B, bytes_accessed=1 << 20, transcendentals=0),
    )(amplitudes, amplitude_mask, integrals, integral_mask, owners.reshape(1, -1))


def solution(mesh):
    Z, Y = mesh.shape["row"] // X, mesh.shape["col"] // 2
    return jax.shard_map(
        functools.partial(per_device, Z, Y),
        mesh=mesh,
        in_specs=(
            P("row", "col", None, None),
            P("row", "col"),
            P("row", "col", None, None),
            P("row", "col"),
            P(),
        ),
        out_specs=P("row", "col", None, None),
        check_vma=False,
    )
```
